32 devices in a mesh: rt: 4 (over x, core), ct: 8 (over z, y).
Axes of the slice: x: 2, y: 2, z: 4, core: 2. Of those that a mesh axis runs over, the one named last changes fastest.
Arguments:
- children: float32 [2048, 12288], P(('rt', 'ct')), may hold values from -6 to 6
- row_map: int32 [2048], replicated, may hold values from 0 to 2047, as said below
- column_map: int32 [2, 12288], replicated, may hold values from 0 to 16383, as said below
- staircase: int32 [2, 48], replicated, may hold values from 640 to 1024, as said below
Outputs:
- factor_rows: float32 [512, 16384], P(None, 'ct')
- basis: float32 [512, 2048], P(None, 'rt')
- remainder: float32 [2048, 16384], P('rt', 'ct')
The draws below stay inside these ranges and needn't reach their ends.
Inputs may be any that keep to these rules, and one draw needn't show every extreme that they name: `row_map`: A permutation of the front rows. Of the 64 stacked child rows in each aligned block of 64 (the rows of one device), at most 32 have front rows in any one aligned block of 512 front rows, and every such block of child rows reaches 32 for some block of front rows. `column_map`: each row is strictly increasing, begins with 0, 1, ..., 511 and ends with 16383. `staircase`: each row is nondecreasing and ends with 1024.
All inputs are finite; a program needn't handle non-finite values.
Results may differ from the reference program's by a relative error of at most 0.0003.
Values sent between devices are 32-bit elements; how exact they have to be, the bound alone decides.
No kernel may reach another device: no remote copies, remote signals or barrier semaphores. Data moves between devices by JAX's collectives and lax.ppermute only.
A program may use at most 128 MiB of HBM per device.

```python
import jax
import jax.numpy as jnp
from jax import lax

FRONT_COLS = 16384
TILE = 256
CHILD_COLS = 12288
PANEL = 512
FRONT_ROWS = 2048
CHILD_ROWS = 1024
SRC_ROWS = 64
CAP = 32
N_RT = 4
N_CT = 8


def shuffle_one(subkey):
    return jax.random.permutation(subkey, SRC_ROWS)


def draw_row_map(key, part):
    sources = N_RT * N_CT
    subkeys = jax.random.split(jax.random.fold_in(key, 101), 3)
    shifts = jax.random.permutation(subkeys[0], sources) % N_RT
    places = jnp.arange(SRC_ROWS, dtype=jnp.int32)
    offsets = jnp.where(places < CAP, 0, (places - CAP) % (N_RT - 1) + 1)
    targets = (shifts[:, None] + offsets[None, :]) % N_RT
    shuffles = jax.vmap(shuffle_one)(jax.random.split(subkeys[1], sources))
    targets = jnp.take_along_axis(targets, shuffles, axis=1).reshape(-1)
    ordering = jax.random.permutation(subkeys[2], FRONT_ROWS)
    grouped = ordering[jnp.argsort(targets[ordering], stable=True)]
    return jnp.zeros((FRONT_ROWS,), jnp.int32).at[grouped].set(jnp.arange(FRONT_ROWS, dtype=jnp.int32))


def one_child(subkey):
    picked = jax.random.permutation(subkey, FRONT_COLS - PANEL - 1)[:CHILD_COLS - PANEL - 1] + PANEL
    return jnp.concatenate([jnp.arange(PANEL, dtype=jnp.int32), jnp.sort(picked).astype(jnp.int32), jnp.full((1,), FRONT_COLS - 1, jnp.int32)])


def draw_column_map(key, part):
    return jax.vmap(one_child)(jax.random.split(jax.random.fold_in(key, 202), 2))


def draw_staircase(key, part):
    tile_count = CHILD_COLS // TILE
    increments = jax.random.randint(jax.random.fold_in(key, 303), (2, tile_count), TILE // 2, 2 * TILE + 1)
    counts = jnp.minimum(PANEL + jnp.cumsum(increments, axis=1), CHILD_ROWS)
    return counts.at[:, tile_count - 1].set(CHILD_ROWS).astype(jnp.int32)


def levels(stream_key, extent, cuts, smallest, largest):
    loudness, own = 1.0, jax.random.fold_in(stream_key, 6)
    for dim, blocks in cuts:
        heights = jnp.exp(jax.random.uniform(jax.random.fold_in(own, dim), (blocks,), jnp.float32, smallest / len(cuts), largest / len(cuts)))
        loudness = loudness * jnp.repeat(heights, extent[dim] // blocks).reshape([-1 if axis == dim else 1 for axis in range(len(extent))])
    return loudness


def gaussian(key, extent, scale, limit, cuts=(), held_as=jnp.bfloat16):
    array = scale * jax.random.normal(key, extent, jnp.float32)
    if cuts:
        array = array * levels(key, extent, cuts, -0.22, 0.18)
    return jnp.clip(array, -limit, limit).astype(held_as)


def setup_inputs(seed: int = 0) -> dict:
    keys = jax.random.split(jax.random.key(seed), 5)
    return {
        "children": gaussian(keys[0], (FRONT_ROWS, CHILD_COLS), 1.0, 6.0, ((0, 32),), jnp.float32),
        "row_map": draw_row_map(jax.random.fold_in(keys[4], 71), 0),
        "column_map": draw_column_map(jax.random.fold_in(keys[4], 71), 0),
        "staircase": draw_staircase(jax.random.fold_in(keys[4], 71), 0),
    }


def householder_upper(panel_cols):
    height = panel_cols.shape[0]
    panel_width = panel_cols.shape[1]
    row_ids = jnp.arange(height, dtype=jnp.int32)

    def reflect(column_index, work_block):
        column = lax.dynamic_index_in_dim(work_block, column_index, 1, keepdims=False)
        column = jnp.where(row_ids >= column_index, column, jnp.zeros_like(column))
        pivot = lax.dynamic_index_in_dim(column, column_index, 0, keepdims=False)
        length = jnp.sqrt(jnp.sum(column * column))
        signed = jnp.where(pivot >= 0, length, -length)
        vector = column + jnp.where(row_ids == column_index, signed, jnp.zeros_like(signed))
        factor = 2.0 / jnp.sum(vector * vector)
        product = jnp.dot(vector, work_block, precision=lax.Precision.HIGHEST)
        return work_block - factor * vector[:, None] * product[None, :]
    work_block = lax.fori_loop(0, panel_width, reflect, panel_cols)
    upper_part = jnp.triu(work_block[:panel_width])
    flips = jnp.where(jnp.diagonal(upper_part) >= 0, 1.0, -1.0).astype(panel_cols.dtype)
    return upper_part * flips[:, None]

def assemble(children, row_map, column_map, staircase):
    total_rows = row_map.shape[0]
    child_rows = total_rows // 2
    within_child = jnp.arange(child_rows, dtype=jnp.int32)
    front_block = jnp.zeros((total_rows, FRONT_COLS), children.dtype)
    for which_child in range(2):
        lower_row = which_child * child_rows
        child_block = children[lower_row:lower_row + child_rows]
        limits = jnp.repeat(staircase[which_child], TILE, total_repeat_length=CHILD_COLS)
        child_block = jnp.where(within_child[:, None] < limits[None, :], child_block, jnp.zeros_like(child_block))
        widened = jnp.zeros((child_rows, FRONT_COLS), children.dtype).at[:, column_map[which_child]].set(child_block)
        front_block = front_block.at[row_map[lower_row:lower_row + child_rows]].set(widened)
    return front_block

def reference(children, row_map, column_map, staircase):
    front_block = assemble(children, row_map, column_map, staircase)
    panel_cols = front_block[:, :PANEL]
    upper_part = householder_upper(panel_cols)
    basis = jax.scipy.linalg.solve_triangular(upper_part.T, panel_cols.T, lower=True)
    factor_rows = jnp.dot(basis, front_block, precision=lax.Precision.HIGHEST)
    removed = lax.dot_general(basis, factor_rows, (((0,), (0,)), ((), ())), precision=lax.Precision.HIGHEST)
    return (factor_rows, basis, front_block - removed)
```

```python
import functools

import jax
import jax.numpy as jnp
import numpy as np
from jax import lax
from jax.experimental import pallas as pl
from jax.experimental.pallas import tpu as pltpu
from jax.sharding import PartitionSpec as P

FRONT_COLS = 16384
PANEL = 512
STEP = 256
LANES = 128
NB = 128
SUB = 8

HI = lax.Precision.HIGHEST
F32 = jnp.float32
BF16 = jnp.bfloat16
MIB = 2**20


def swap(x, rt_bit, ct_bit):
    n_rt, n_ct = lax.axis_size("rt"), lax.axis_size("ct")
    if not rt_bit:
        return lax.ppermute(x, "ct", [(c, c ^ ct_bit) for c in range(n_ct)])
    if not ct_bit:
        return lax.ppermute(x, "rt", [(r, r ^ rt_bit) for r in range(n_rt)])
    pairs = [
        (r * n_ct + c, (r ^ rt_bit) * n_ct + (c ^ ct_bit)) for r in range(n_rt) for c in range(n_ct)
    ]
    return lax.ppermute(x, ("rt", "ct"), pairs)


def bits_down(size, last):
    bit, bits = size // 2, []
    while bit >= last:
        bits.append(bit)
        bit //= 2
    return bits


def combos(bits):
    order = [0]
    for bit in bits:
        order = order + [value ^ bit for value in order]
    return order


def halves(x):
    high = x.astype(BF16)
    return high, (x - high.astype(F32)).astype(BF16)


def dot(a, b):
    return jnp.dot(a, b, preferred_element_type=F32)


def dot_nt(a, b, precision=None):
    return lax.dot_general(
        a, b, (((1,), (1,)), ((), ())), precision=precision, preferred_element_type=F32
    )


def dot_tn(a, b, precision=None):
    return lax.dot_general(
        a, b, (((0,), (0,)), ((), ())), precision=precision, preferred_element_type=F32
    )


def params(mib):
    return pltpu.CompilerParams(vmem_limit_bytes=mib * MIB)


def widen_kernel(tiles, window, info, child, cmap, limits, *outs):
    rows = child.shape[0]
    my_block = info[info.shape[0] - 2]
    first_row = info[info.shape[0] - 1]
    row_ids = first_row + lax.broadcasted_iota(jnp.int32, (rows, window), 0)
    col_ids = lax.broadcasted_iota(jnp.int32, (STEP, window), 0)
    for place, out in enumerate(outs):
        block = my_block ^ place

        def tile(i, carry, block=block, out=out):
            t = block * tiles + i
            cols = pl.ds(pl.multiple_of(info[t] * LANES, LANES), window)
            live = jnp.where(row_ids < limits[:, cols], child[:, cols], 0.0)
            hot = jnp.where(col_ids + t * STEP == cmap[:, cols], 1.0, 0.0).astype(BF16)
            high = live.astype(BF16)
            rest = live - high.astype(F32)
            mid = rest.astype(BF16)
            low = (rest - mid.astype(F32)).astype(BF16)
            spread = dot_nt(jnp.concatenate([high, mid, low], axis=0), hot)
            out[:, pl.ds(pl.multiple_of(i * STEP, STEP), STEP)] = (
                spread[:rows] + spread[rows : 2 * rows] + spread[2 * rows :]
            )
            return carry

        lax.fori_loop(0, tiles, tile, 0)


def widen(info, child, cmap, limits, n_ct):
    rows, width = child.shape
    block_cols = FRONT_COLS // n_ct
    window = STEP + LANES
    whole = pl.BlockSpec(memory_space=pltpu.VMEM)
    return pl.pallas_call(
        functools.partial(widen_kernel, block_cols // STEP, window),
        out_shape=[jax.ShapeDtypeStruct((rows, block_cols), F32)] * n_ct,
        in_specs=[pl.BlockSpec(memory_space=pltpu.SMEM), whole, whole, whole],
        out_specs=[whole] * n_ct,
        compiler_params=params(24),
        cost_estimate=pl.CostEstimate(
            flops=6 * rows * window * FRONT_COLS,
            bytes_accessed=4 * rows * (width + FRONT_COLS),
            transcendentals=0,
        ),
    )(info, child, cmap, limits)


def small_inverse(tile):
    a = [
        [jnp.broadcast_to(tile[i : i + 1, k : k + 1], (SUB, NB)) for k in range(i + 1)]
        for i in range(SUB)
    ]
    scale = [None] * SUB
    lower = [[None] * SUB for _ in range(SUB)]
    inverse = [[None] * SUB for _ in range(SUB)]
    for j in range(SUB):
        scale[j] = lax.rsqrt(a[j][j])
        for i in range(j + 1, SUB):
            lower[i][j] = a[i][j] * scale[j]
        for i in range(j + 1, SUB):
            for k in range(j + 1, i + 1):
                a[i][k] = a[i][k] - lower[i][j] * lower[k][j]
    for j in range(SUB):
        inverse[j][j] = scale[j]
        for i in range(j + 1, SUB):
            total = lower[i][j] * inverse[j][j]
            for k in range(j + 1, i):
                total = total + lower[i][k] * inverse[k][j]
            inverse[i][j] = -scale[i] * total
    return inverse


def apply_small(inverse, tiles):
    sub = lax.broadcasted_iota(jnp.int32, (SUB, NB), 0)
    outs = [None] * len(tiles)
    for k in range(SUB):
        column = jnp.zeros((SUB, NB), F32)
        for i in range(k, SUB):
            column = jnp.where(sub == i, inverse[i][k], column)
        for n, tile in enumerate(tiles):
            term = column * jnp.broadcast_to(tile[k : k + 1, :], (SUB, NB))
            outs[n] = term if outs[n] is None else outs[n] + term
    return outs


def identity(n):
    shape = (n, n)
    same = lax.broadcasted_iota(jnp.int32, shape, 0) == lax.broadcasted_iota(jnp.int32, shape, 1)
    return jnp.where(same, 1.0, 0.0)


def diagonal_inverse(block, out):
    lane = lax.broadcasted_iota(jnp.int32, (SUB, NB), 1)

    def body(s, carry):
        work, right = carry
        inverse = small_inverse(work[:SUB])
        top, top_right = apply_small(inverse, [work[:SUB], right[:SUB]])
        out[pl.ds(pl.multiple_of(SUB * s, SUB), SUB), :] = top_right
        top = jnp.where(lane < NB - SUB * s, top, 0.0)
        change = dot_tn(top, jnp.concatenate([top, top_right], axis=1), HI)
        work = work - change[:, :NB]
        right = right - change[:, NB:]
        work = pltpu.roll(jnp.concatenate([work[SUB:], work[:SUB]], axis=0), NB - SUB, 1)
        right = jnp.concatenate([right[SUB:], right[:SUB]], axis=0)
        return work, right

    lax.fori_loop(0, NB // SUB, body, (block, identity(NB)))


def factor_kernel(gram_a, gram_b, out, work, small):
    n = gram_a.shape[0]
    work[:, :n] = gram_a[...] + gram_b[...]
    work[:, n:] = identity(n)
    for lo in range(0, n, NB):
        hi = lo + NB
        diagonal_inverse(work[lo:hi, lo:hi], small)
        rows = jnp.dot(small[...], work[lo:hi, lo : n + hi], precision=HI, preferred_element_type=F32)
        out[lo:hi, :hi] = rows[:, n - lo :]
        if hi < n:
            out[lo:hi, hi:] = jnp.zeros((NB, n - hi), F32)
            work[hi:, hi : n + hi] -= dot_tn(rows[:, NB : n - lo], rows[:, NB:], HI)


def inverse_factor(gram_a, gram_b):
    n = gram_a.shape[0]
    return pl.pallas_call(
        factor_kernel,
        out_shape=jax.ShapeDtypeStruct((n, n), F32),
        scratch_shapes=[pltpu.VMEM((n, 2 * n), F32), pltpu.VMEM((NB, NB), F32)],
        compiler_params=params(24),
        cost_estimate=pl.CostEstimate(
            flops=40 * 10**9, bytes_accessed=12 * n * n, transcendentals=0
        ),
    )(gram_a, gram_b)


def basis_kernel(inverse, own, other, targets, q_high, q_low, basis, turned_high, turned_low):
    d = pl.program_id(0)
    group, panel = targets.shape[-1], inverse.shape[0]
    rows = jnp.concatenate(
        [own[...].reshape(group // 2, panel), other[...].reshape(group // 2, panel)], axis=0
    )
    inv_high, inv_low = halves(inverse[...])
    high, low = halves(rows)
    q = dot_nt(inv_high, high) + (dot_nt(inv_low, high) + dot_nt(inv_high, low))
    q_h, q_l = halves(q)
    q_high[...] = q_h
    q_low[...] = q_l
    front = basis.shape[1]
    ids = lax.broadcasted_iota(jnp.int32, (front, group), 0)
    hot = jnp.where(ids == targets[0], 1.0, 0.0).astype(BF16)
    part = dot_nt(q_h, hot) + dot_nt(q_l, hot)

    @pl.when(d == 0)
    def _():
        basis[...] = part

    @pl.when(d > 0)
    def _():
        basis[...] += part

    @pl.when(d == pl.num_programs(0) - 1)
    def _():
        turned_h, turned_l = halves(basis[...].T)
        turned_high[...] = turned_h
        turned_low[...] = turned_l


def basis_rows(inverse, own, other, targets, front_rows):
    half, n_ct, src, panel = own.shape
    group = 2 * half * src
    depth = n_ct.bit_length() - 1

    def place(d):
        return (0, sum(((d >> k) & 1) << (depth - 1 - k) for k in range(depth)), 0, 0)

    wide = jax.ShapeDtypeStruct((panel, n_ct * group), BF16)
    return pl.pallas_call(
        basis_kernel,
        grid=(n_ct,),
        out_shape=[
            wide,
            wide,
            jax.ShapeDtypeStruct((panel, front_rows), F32),
            jax.ShapeDtypeStruct((front_rows, panel), BF16),
            jax.ShapeDtypeStruct((front_rows, panel), BF16),
        ],
        in_specs=[
            pl.BlockSpec((panel, panel), lambda d: (0, 0)),
            pl.BlockSpec((half, 1, src, panel), place),
            pl.BlockSpec((half, 1, src, panel), place),
            pl.BlockSpec((1, 1, group), lambda d: (d, 0, 0)),
        ],
        out_specs=[
            pl.BlockSpec((panel, group), lambda d: (0, d)),
            pl.BlockSpec((panel, group), lambda d: (0, d)),
            pl.BlockSpec((panel, front_rows), lambda d: (0, 0)),
            pl.BlockSpec((front_rows, panel), lambda d: (0, 0)),
            pl.BlockSpec((front_rows, panel), lambda d: (0, 0)),
        ],
        compiler_params=params(24),
        cost_estimate=pl.CostEstimate(
            flops=10 * panel * panel * n_ct * group, bytes_accessed=12 * MIB, transcendentals=0
        ),
    )(inverse, own, other, targets)


def mix(q_high, q_low, hot, pieces):
    rows = jnp.concatenate([piece[...] for piece in pieces], axis=0)
    high, low = halves(rows)
    factor = dot(q_high[...], high) + (dot(q_low[...], high) + dot(q_high[...], low))
    return factor, dot(hot[...], high) + dot(hot[...], low)


def build_hot(targets, hot):
    @pl.when(pl.program_id(0) == 0)
    def _():
        ids = lax.broadcasted_iota(jnp.int32, hot.shape, 0)
        hot[...] = jnp.where(ids == targets[...], 1.0, 0.0).astype(BF16)


def first_kernel(count, q_high, q_low, targets, *refs):
    pieces, (factor, placed, hot) = refs[:count], refs[count:]
    build_hot(targets, hot)
    factor[...], placed[...] = mix(q_high, q_low, hot, pieces)


def more_kernel(count, q_high, q_low, targets, factor_in, placed_in, *refs):
    pieces, (factor, placed, hot) = refs[:count], refs[count:]
    build_hot(targets, hot)
    add_factor, add_placed = mix(q_high, q_low, hot, pieces)
    factor[...] = factor_in[...] + add_factor
    placed[...] = placed_in[...] + add_placed


def last_kernel(count, q_high, q_low, targets, factor_in, placed_in, turned_high, turned_low, *refs):
    pieces, (factor, remainder, hot) = refs[:count], refs[count:]
    build_hot(targets, hot)
    add_factor, add_placed = mix(q_high, q_low, hot, pieces)
    total = factor_in[...] + add_factor
    factor[...] = total
    high, low = halves(total)
    removed = dot(turned_high[...], high) + (dot(turned_low[...], high) + dot(turned_high[...], low))
    remainder[...] = (placed_in[...] + add_placed) - removed


def mix_call(kernel, q_high, q_low, targets, group, extra, turned, pieces, front_rows):
    panel = q_high.shape[0]
    src, block_cols = pieces[0].shape
    depth = len(pieces) * src
    column = lambda j: (0, j)
    fixed = lambda j: (0, group)
    still = lambda j: (0, 0)
    flops = 2 * depth * block_cols * (3 * panel + 2 * front_rows)
    flops += 6 * panel * front_rows * block_cols if turned else 0
    return pl.pallas_call(
        functools.partial(kernel, len(pieces)),
        grid=(block_cols // STEP,),
        out_shape=[
            jax.ShapeDtypeStruct((panel, block_cols), F32),
            jax.ShapeDtypeStruct((front_rows, block_cols), F32),
        ],
        in_specs=[
            pl.BlockSpec((panel, depth), fixed),
            pl.BlockSpec((panel, depth), fixed),
            pl.BlockSpec((1, depth), fixed),
        ]
        + [pl.BlockSpec((x.shape[0], STEP), column) for x in extra]
        + [pl.BlockSpec(x.shape, still) for x in turned]
        + [pl.BlockSpec((src, STEP), column) for _ in pieces],
        out_specs=[
            pl.BlockSpec((panel, STEP), column),
            pl.BlockSpec((front_rows, STEP), column),
        ],
        scratch_shapes=[pltpu.VMEM((front_rows, depth), BF16)],
        compiler_params=params(32),
        cost_estimate=pl.CostEstimate(
            flops=flops,
            bytes_accessed=4 * block_cols * (depth + (1 + bool(extra)) * (panel + front_rows)),
            transcendentals=0,
        ),
    )(q_high, q_low, targets, *extra, *turned, *pieces)


def shards(children, row_map, column_map, staircase):
    n_rt, n_ct = lax.axis_size("rt"), lax.axis_size("ct")
    my_rt, my_ct = lax.axis_index("rt"), lax.axis_index("ct")
    src, child_cols = children.shape
    total_rows = row_map.shape[0]
    child_rows = total_rows // 2
    front_rows = total_rows // n_rt
    tile_cols = child_cols // staircase.shape[1]
    n_dev = n_rt * n_ct

    first_row = (my_rt * n_ct + my_ct) * src
    which = first_row // child_rows
    first_within = first_row - which * child_rows
    cmap = lax.dynamic_index_in_dim(column_map, which, 0, keepdims=False)
    stairs = lax.dynamic_index_in_dim(staircase, which, 0, keepdims=False)
    limits = jnp.broadcast_to(stairs[:, None], (stairs.shape[0], tile_cols)).reshape(-1)

    within = first_within + jnp.arange(src, dtype=jnp.int32)
    panel = jnp.where(within[:, None] < limits[None, :PANEL], children[:, :PANEL], 0.0)
    ct_bits, rt_bits = bits_down(n_ct, 1), bits_down(n_rt, 2)
    for bit in ct_bits:
        panel = jnp.concatenate([panel, swap(panel, 0, bit)], axis=0)
    for bit in rt_bits:
        panel = jnp.concatenate([panel, swap(panel, bit, 0)], axis=0)
    gram = dot_tn(panel, panel, HI)
    other_gram = swap(gram, 1, 0)
    other_panel = swap(panel, 1, 0)

    rt_order = combos(rt_bits)
    rt_order = rt_order + [r ^ 1 for r in rt_order]
    sources = (my_rt ^ np.array(rt_order, np.int32))[None, :] * n_ct + (
        my_ct ^ np.arange(n_ct, dtype=np.int32)
    )[:, None]
    targets = row_map.reshape(n_dev, src)[sources.reshape(-1)] - my_rt * front_rows
    targets = targets.reshape(n_ct, 1, n_rt * src)
    flat_targets = targets.reshape(1, total_rows)

    edges = STEP * jnp.arange(FRONT_COLS // STEP, dtype=jnp.int32)
    starts = jnp.sum((cmap[None, :] < edges[:, None]).astype(jnp.int32), axis=1)
    starts = jnp.minimum(starts // LANES, (child_cols - STEP - LANES) // LANES)
    info = jnp.concatenate([starts, my_ct[None], first_within[None]]).astype(jnp.int32)
    blocks = widen(info, children, cmap[None, :], limits[None, :], n_ct)

    pieces = [None] * n_ct
    for d in list(range(n_ct // 2, n_ct)) + list(range(n_ct // 2)):
        mine = [swap(blocks[d], 0, d) if d else blocks[0]]
        for bit in rt_bits + [1]:
            mine = mine + [swap(x, bit, 0) for x in mine]
        pieces[d] = mine

    inverse = inverse_factor(gram, other_gram)
    half = n_rt // 2
    q_high, q_low, basis, turned_high, turned_low = basis_rows(
        inverse,
        panel.reshape(half, n_ct, src, PANEL),
        other_panel.reshape(half, n_ct, src, PANEL),
        targets,
        front_rows,
    )
    call = functools.partial(mix_call, front_rows=front_rows)
    two, four = n_ct // 2, n_ct // 4
    gather = lambda lo, hi: [x for d in range(lo, hi) for x in pieces[d]]
    state = call(first_kernel, q_high, q_low, flat_targets, 0, (), (), gather(0, two))
    state = call(more_kernel, q_high, q_low, flat_targets, 2, tuple(state), (), gather(two, two + four))
    factor, remainder = call(
        last_kernel,
        q_high,
        q_low,
        flat_targets,
        3,
        tuple(state),
        (turned_high, turned_low),
        gather(two + four, n_ct),
    )
    return factor, basis, remainder


def solution(mesh):
    placed = (P(("rt", "ct"), None), P(), P(), P())
    return jax.shard_map(
        shards,
        mesh=mesh,
        in_specs=placed,
        out_specs=(P(None, "ct"), P(None, "rt"), P("rt", "ct")),
        check_vma=False,
    )
```

```python
import functools

import jax
import jax.numpy as jnp
import numpy as np
from jax import lax
from jax.experimental import pallas as pl
from jax.experimental.pallas import tpu as pltpu
from jax.sharding import PartitionSpec as P

FRONT_COLS = 16384
PANEL = 512
STEP = 256
WIDE = 512
LANES = 128
NB = 128
SUB = 8

HI = lax.Precision.HIGHEST
F32 = jnp.float32
BF16 = jnp.bfloat16
MIB = 2**20


def swap(x, rt_bit, ct_bit):
    n_rt, n_ct = lax.axis_size("rt"), lax.axis_size("ct")
    if not rt_bit:
        return lax.ppermute(x, "ct", [(c, c ^ ct_bit) for c in range(n_ct)])
    if not ct_bit:
        return lax.ppermute(x, "rt", [(r, r ^ rt_bit) for r in range(n_rt)])
    pairs = [
        (r * n_ct + c, (r ^ rt_bit) * n_ct + (c ^ ct_bit)) for r in range(n_rt) for c in range(n_ct)
    ]
    return lax.ppermute(x, ("rt", "ct"), pairs)


def bits_down(size, last):
    bit, bits = size // 2, []
    while bit >= last:
        bits.append(bit)
        bit //= 2
    return bits


def combos(bits):
    order = [0]
    for bit in bits:
        order = order + [value ^ bit for value in order]
    return order


def halves(x):
    high = x.astype(BF16)
    return high, (x - high.astype(F32)).astype(BF16)


def dot(a, b):
    return jnp.dot(a, b, preferred_element_type=F32)


def dot_nt(a, b, precision=None):
    return lax.dot_general(
        a, b, (((1,), (1,)), ((), ())), precision=precision, preferred_element_type=F32
    )


def dot_tn(a, b, precision=None):
    return lax.dot_general(
        a, b, (((0,), (0,)), ((), ())), precision=precision, preferred_element_type=F32
    )


MARK = jax.ShapeDtypeStruct((SUB, LANES), F32)


def params(mib):
    return pltpu.CompilerParams(vmem_limit_bytes=mib * MIB)


def widen_kernel(tiles, window, places, waits, info, child, cmap, limits, *outs):
    rows = child.shape[0]
    my_block = info[info.shape[0] - 2]
    first_row = info[info.shape[0] - 1]
    row_ids = first_row + lax.broadcasted_iota(jnp.int32, (rows, window), 0)
    col_ids = lax.broadcasted_iota(jnp.int32, (STEP, window), 0)
    for place, out in zip(places, outs[waits:-1]):
        block = my_block ^ place

        def tile(i, carry, block=block, out=out):
            t = block * tiles + i
            cols = pl.ds(pl.multiple_of(info[t] * LANES, LANES), window)
            live = jnp.where(row_ids < limits[:, cols], child[:, cols], 0.0)
            hot = jnp.where(col_ids == cmap[:, cols] - t * STEP, 1.0, 0.0).astype(BF16)
            spread = dot_nt(jnp.concatenate(halves(live), axis=0), hot)
            out[:, pl.ds(pl.multiple_of(i * STEP, STEP), STEP)] = spread[:rows] + spread[rows:]
            return carry

        lax.fori_loop(0, tiles, tile, 0, unroll=4)


def widen(info, child, cmap, limits, places, n_ct, tokens):
    rows, width = child.shape
    block_cols = FRONT_COLS // n_ct
    window = STEP + LANES
    whole = pl.BlockSpec(memory_space=pltpu.VMEM)
    made = pl.pallas_call(
        functools.partial(widen_kernel, block_cols // STEP, window, tuple(places), len(tokens)),
        out_shape=[jax.ShapeDtypeStruct((rows, block_cols), F32)] * len(places) + [MARK],
        in_specs=[pl.BlockSpec(memory_space=pltpu.SMEM), whole, whole, whole]
        + [pl.BlockSpec(memory_space=pl.ANY)] * len(tokens),
        out_specs=[whole] * len(places) + [pl.BlockSpec(memory_space=pl.ANY)],
        compiler_params=params(56),
        cost_estimate=pl.CostEstimate(
            flops=4 * rows * window * block_cols * len(places),
            bytes_accessed=4 * rows * (width + block_cols * len(places)),
            transcendentals=0,
        ),
    )(info, child, cmap, limits, *tokens)
    return dict(zip(places, made)), made[-1]


def small_inverse(tile):
    a = [
        [jnp.broadcast_to(tile[i : i + 1, k : k + 1], (SUB, NB)) for k in range(i + 1)]
        for i in range(SUB)
    ]
    scale = [None] * SUB
    lower = [[None] * SUB for _ in range(SUB)]
    inverse = [[None] * SUB for _ in range(SUB)]
    for j in range(SUB):
        scale[j] = lax.rsqrt(a[j][j])
        for i in range(j + 1, SUB):
            lower[i][j] = a[i][j] * scale[j]
        for i in range(j + 1, SUB):
            for k in range(j + 1, i + 1):
                a[i][k] = a[i][k] - lower[i][j] * lower[k][j]
    for j in range(SUB):
        inverse[j][j] = scale[j]
        for i in range(j + 1, SUB):
            total = lower[i][j] * inverse[j][j]
            for k in range(j + 1, i):
                total = total + lower[i][k] * inverse[k][j]
            inverse[i][j] = -scale[i] * total
    return inverse


def apply_small(inverse, tiles):
    sub = lax.broadcasted_iota(jnp.int32, (SUB, NB), 0)
    outs = [None] * len(tiles)
    for k in range(SUB):
        column = jnp.zeros((SUB, NB), F32)
        for i in range(k, SUB):
            column = jnp.where(sub == i, inverse[i][k], column)
        for n, tile in enumerate(tiles):
            term = column * jnp.broadcast_to(tile[k : k + 1, :], (SUB, NB))
            outs[n] = term if outs[n] is None else outs[n] + term
    return outs


def identity(n):
    shape = (n, n)
    same = lax.broadcasted_iota(jnp.int32, shape, 0) == lax.broadcasted_iota(jnp.int32, shape, 1)
    return jnp.where(same, 1.0, 0.0)


def thirds(x):
    high = x.astype(BF16)
    rest = x - high.astype(F32)
    mid = rest.astype(BF16)
    return high, mid, (rest - mid.astype(F32)).astype(BF16)


def diagonal_inverse(block, out, work):
    lane = lax.broadcasted_iota(jnp.int32, (SUB, NB), 1)
    work[:NB, :NB] = block
    work[:NB, NB:] = identity(NB)
    work[NB:, :] = jnp.zeros((SUB, 2 * NB), F32)

    def body(s, carry):
        tile, before = carry
        h, m, l = thirds(before)
        left = jnp.concatenate([x[:, :NB] for x in (h, h, m, h, l, m)], axis=0)
        right = jnp.concatenate([h, m, h, l, h, m], axis=0)
        work[:NB, :] = work[:NB, :] - dot_tn(left, right)
        after = work[pl.ds(pl.multiple_of(SUB * s + SUB, SUB), SUB), :]
        shift = lax.rem(NB - SUB * s, NB)
        inverse = small_inverse(pltpu.roll(tile[:, :NB], shift, 1))
        turned = pltpu.roll(after[:, :NB], shift, 1)
        top, top_right = apply_small(inverse, [tile[:, :NB], tile[:, NB:]])
        out[pl.ds(pl.multiple_of(SUB * s, SUB), SUB), :] = top_right
        top = jnp.concatenate([jnp.where(lane >= SUB * s, top, 0.0), top_right], axis=1)
        columns = [jnp.broadcast_to(turned[:, k : k + 1], (SUB, NB)) for k in range(SUB)]
        for i in range(SUB):
            weight = inverse[i][0] * columns[0]
            for k in range(1, i + 1):
                weight = weight + inverse[i][k] * columns[k]
            weight = jnp.concatenate([weight, weight], axis=1)
            after = after - weight * jnp.broadcast_to(top[i : i + 1], (SUB, 2 * NB))
        return after, top

    lax.fori_loop(0, NB // SUB, body, (work[:SUB, :], jnp.zeros((SUB, 2 * NB), F32)))


def factor_kernel(gram_a, gram_b, *refs):
    out, _, whole, small, work = refs[-5:]
    n = out.shape[0]
    whole[:, :n] = gram_a[...] + gram_b[...]
    whole[:, n:] = identity(n)
    for lo in range(0, n, NB):
        hi = lo + NB
        diagonal_inverse(whole[lo:hi, lo:hi], small, work)
        rows = jnp.dot(small[...], whole[lo:hi, lo : n + hi], precision=HI, preferred_element_type=F32)
        out[lo:hi, :hi] = rows[:, n - lo :]
        if hi < n:
            out[lo:hi, hi:] = jnp.zeros((NB, n - hi), F32)
            whole[hi:, hi : n + hi] -= dot_tn(rows[:, NB : n - lo], rows[:, NB:], HI)


def inverse_factor(gram_a, gram_b, tokens):
    n = gram_a.shape[0]
    whole = pl.BlockSpec(memory_space=pltpu.VMEM)
    return pl.pallas_call(
        factor_kernel,
        out_shape=[jax.ShapeDtypeStruct((n, n), F32), MARK],
        in_specs=[whole] * 2 + [pl.BlockSpec(memory_space=pl.ANY)] * len(tokens),
        out_specs=[whole, pl.BlockSpec(memory_space=pl.ANY)],
        scratch_shapes=[
            pltpu.VMEM((n, 2 * n), F32),
            pltpu.VMEM((NB, NB), F32),
            pltpu.VMEM((NB + SUB, 2 * NB), F32),
        ],
        compiler_params=params(56),
        cost_estimate=pl.CostEstimate(
            flops=30 * 10**9, bytes_accessed=12 * n * n, transcendentals=0
        ),
    )(gram_a, gram_b, *tokens)


def gate_kernel(*refs):
    pass


def gate(arrays, tokens):
    if not arrays:
        return []
    anywhere = pl.BlockSpec(memory_space=pl.ANY)
    return pl.pallas_call(
        gate_kernel,
        out_shape=[jax.ShapeDtypeStruct(x.shape, x.dtype) for x in arrays],
        in_specs=[anywhere] * (len(arrays) + len(tokens)),
        out_specs=[anywhere] * len(arrays),
        input_output_aliases={k: k for k in range(len(arrays))},
        cost_estimate=pl.CostEstimate(flops=0, bytes_accessed=0, transcendentals=0),
    )(*arrays, *tokens)


def join_kernel(count, cut, *refs):
    parts, outs = refs[:count], refs[-cut - 1 : -1]
    width = outs[0].shape[1]
    row = 0
    for part in parts:
        rows = part.shape[0]
        for k, out in enumerate(outs):
            out[row : row + rows, :] = part[:, k * width : (k + 1) * width]
        row += rows


def join(parts, tokens=(), cut=1):
    rows, width = sum(x.shape[0] for x in parts), parts[0].shape[1]
    whole = pl.BlockSpec(memory_space=pltpu.VMEM)
    out = pl.pallas_call(
        functools.partial(join_kernel, len(parts), cut),
        out_shape=[jax.ShapeDtypeStruct((rows, width // cut), F32)] * cut + [MARK],
        in_specs=[whole] * len(parts) + [pl.BlockSpec(memory_space=pl.ANY)] * len(tokens),
        out_specs=[whole] * cut + [pl.BlockSpec(memory_space=pl.ANY)],
        compiler_params=params(16 if width == PANEL or width == PANEL // 2 else 56),
        cost_estimate=pl.CostEstimate(
            flops=0, bytes_accessed=8 * rows * width, transcendentals=0
        ),
    )(*parts, *tokens)
    return (out[:cut] if cut > 1 else out[0]), out[-1]


def gram_kernel(a_mine, a_other, b_mine, b_other, *refs):
    panel, gram = refs[-3:-1]
    half, width = a_mine.shape
    quarter = half // 2
    panel[:half, :width] = a_mine[...]
    panel[half:, :width] = a_other[...]
    for k, source in enumerate((b_mine, b_other)):
        panel[k * quarter : (k + 1) * quarter, width:] = source[:quarter, :]
        panel[half + k * quarter : half + (k + 1) * quarter, width:] = source[quarter:, :]
    rows = panel[...]
    gram[...] = dot_tn(rows, rows, HI)


def gram_of(a_mine, a_other, b_mine, b_other, tokens):
    half, width = a_mine.shape
    whole = pl.BlockSpec(memory_space=pltpu.VMEM)
    return pl.pallas_call(
        gram_kernel,
        out_shape=[
            jax.ShapeDtypeStruct((2 * half, 2 * width), F32),
            jax.ShapeDtypeStruct((2 * width, 2 * width), F32),
            MARK,
        ],
        in_specs=[whole] * 4 + [pl.BlockSpec(memory_space=pl.ANY)] * len(tokens),
        out_specs=[whole] * 2 + [pl.BlockSpec(memory_space=pl.ANY)],
        compiler_params=params(24),
        cost_estimate=pl.CostEstimate(
            flops=4 * half * 4 * width * width, bytes_accessed=4 * half * width, transcendentals=0
        ),
    )(a_mine, a_other, b_mine, b_other, *tokens)


def basis_kernel(count, waits, *refs):
    inverse, refs = refs[:count], refs[count:]
    own, other, targets = refs[:3]
    q_high, q_low, basis, turned_high, turned_low = refs[3 + waits :]
    d = pl.program_id(0)
    group, panel = targets.shape[-1], inverse[0].shape[1]
    rows = jnp.concatenate(
        [own[...].reshape(group // 2, panel), other[...].reshape(group // 2, panel)], axis=0
    )
    inv_high, inv_low = halves(inverse[0][...])
    high, low = halves(rows)
    q = dot_nt(inv_high, high) + (dot_nt(inv_low, high) + dot_nt(inv_high, low))
    q_h, q_l = halves(q)
    q_high[...] = q_h
    q_low[...] = q_l
    front = basis.shape[1]
    ids = lax.broadcasted_iota(jnp.int32, (front, group), 0)
    hot = jnp.where(ids == targets[0], 1.0, 0.0).astype(BF16)
    part = dot_nt(q_h, hot) + dot_nt(q_l, hot)

    @pl.when(d == 0)
    def _():
        basis[...] = part

    @pl.when(d > 0)
    def _():
        basis[...] += part

    @pl.when(d == pl.num_programs(0) - 1)
    def _():
        turned_h, turned_l = halves(basis[...].T)
        turned_high[...] = turned_h
        turned_low[...] = turned_l


def basis_rows(inverse, own, other, targets, tokens, front_rows, order):
    last, half, upper, src, panel = own.shape
    n_ct = last * upper
    group = 2 * half * src
    depth = upper.bit_length() - 1

    def place(step):
        d = sum(jnp.where(step == k, value, 0) for k, value in enumerate(order))
        spot = sum(((d >> (k + 1)) & 1) << (depth - 1 - k) for k in range(depth))
        return (d & 1, 0, spot, 0, 0)

    wide = jax.ShapeDtypeStruct((panel, n_ct * group), BF16)
    return pl.pallas_call(
        functools.partial(basis_kernel, len(inverse), len(tokens)),
        grid=(n_ct,),
        out_shape=[
            wide,
            wide,
            jax.ShapeDtypeStruct((panel, front_rows), F32),
            jax.ShapeDtypeStruct((front_rows, panel), BF16),
            jax.ShapeDtypeStruct((front_rows, panel), BF16),
        ],
        in_specs=[
            *[pl.BlockSpec((panel, panel), lambda d: (0, 0)) for _ in inverse],
            pl.BlockSpec((1, half, 1, src, panel), place),
            pl.BlockSpec((1, half, 1, src, panel), place),
            pl.BlockSpec((1, 1, group), lambda d: (d, 0, 0)),
            *[pl.BlockSpec(memory_space=pl.ANY) for _ in tokens],
        ],
        out_specs=[
            pl.BlockSpec((panel, group), lambda d: (0, d)),
            pl.BlockSpec((panel, group), lambda d: (0, d)),
            pl.BlockSpec((panel, front_rows), lambda d: (0, 0)),
            pl.BlockSpec((front_rows, panel), lambda d: (0, 0)),
            pl.BlockSpec((front_rows, panel), lambda d: (0, 0)),
        ],
        compiler_params=params(56),
        cost_estimate=pl.CostEstimate(
            flops=8 * panel * panel * n_ct * group, bytes_accessed=6 * MIB, transcendentals=0
        ),
    )(*inverse, own, other, targets, *tokens)


def mix(q_high, q_low, hot, pieces, spots, src):
    rows = jnp.concatenate([pieces[n][lo : lo + src, :] for n, lo in spots], axis=0)
    high, low = halves(rows)
    factor = dot(q_high[...], high) + (dot(q_low[...], high) + dot(q_high[...], low))
    return factor, dot(hot[...], high) + dot(hot[...], low)


def build_hot(targets, hot):
    @pl.when(pl.program_id(0) == 0)
    def _():
        ids = lax.broadcasted_iota(jnp.int32, hot.shape, 0)
        hot[...] = jnp.where(ids == targets[...], 1.0, 0.0).astype(BF16)


def first_kernel(count, spots, src, q_high, q_low, targets, *refs):
    pieces, (factor, placed, hot) = refs[:count], refs[-3:]
    build_hot(targets, hot)
    factor[...], placed[...] = mix(q_high, q_low, hot, pieces, spots, src)


def more_kernel(count, spots, src, q_high, q_low, targets, factor_in, placed_in, *refs):
    pieces, (factor, placed, hot) = refs[:count], refs[-3:]
    build_hot(targets, hot)
    add_factor, add_placed = mix(q_high, q_low, hot, pieces, spots, src)
    factor[...] = factor_in[...] + add_factor
    placed[...] = placed_in[...] + add_placed


def last_kernel(count, spots, src, q_high, q_low, targets, factor_in, placed_in, turned_high, turned_low, *refs):
    pieces, (factor, remainder, hot) = refs[:count], refs[-3:]
    build_hot(targets, hot)
    add_factor, add_placed = mix(q_high, q_low, hot, pieces, spots, src)
    total = factor_in[...] + add_factor
    factor[...] = total
    high, low = halves(total)
    removed = dot(turned_high[...], high) + (dot(turned_low[...], high) + dot(turned_high[...], low))
    remainder[...] = (placed_in[...] + add_placed) - removed


def mix_call(kernel, group, extra, turned, pieces, spots, q_high, q_low, targets, src, front_rows, tokens):
    panel = q_high.shape[0]
    block_cols = pieces[0].shape[1]
    depth = len(spots) * src
    column = lambda j: (0, j)
    fixed = lambda j: (0, group)
    still = lambda j: (0, 0)
    flops = depth * block_cols * (3 * panel + 2 * front_rows)
    flops += 3 * panel * front_rows * block_cols if turned else 0
    return pl.pallas_call(
        functools.partial(kernel, len(pieces), spots, src),
        grid=(block_cols // WIDE,),
        out_shape=[
            jax.ShapeDtypeStruct((panel, block_cols), F32),
            jax.ShapeDtypeStruct((front_rows, block_cols), F32),
        ],
        in_specs=[
            pl.BlockSpec((panel, depth), fixed),
            pl.BlockSpec((panel, depth), fixed),
            pl.BlockSpec((1, depth), fixed),
        ]
        + [pl.BlockSpec((x.shape[0], WIDE), column) for x in extra]
        + [pl.BlockSpec(x.shape, still) for x in turned]
        + [pl.BlockSpec((x.shape[0], WIDE), column) for x in pieces]
        + [pl.BlockSpec(memory_space=pl.ANY)] * len(tokens),
        out_specs=[
            pl.BlockSpec((panel, WIDE), column),
            pl.BlockSpec((front_rows, WIDE), column),
        ],
        scratch_shapes=[pltpu.VMEM((front_rows, depth), BF16)],
        compiler_params=params(56),
        cost_estimate=pl.CostEstimate(
            flops=flops,
            bytes_accessed=block_cols * (depth + (1 + bool(extra)) * (panel + front_rows)),
            transcendentals=0,
        ),
    )(q_high, q_low, targets, *extra, *turned, *pieces, *tokens)


def shards(children, row_map, column_map, staircase):
    n_rt, n_ct = lax.axis_size("rt"), lax.axis_size("ct")
    my_rt, my_ct = lax.axis_index("rt"), lax.axis_index("ct")
    src, child_cols = children.shape
    total_rows = row_map.shape[0]
    child_rows = total_rows // 2
    front_rows = total_rows // n_rt
    tile_cols = child_cols // staircase.shape[1]
    n_dev = n_rt * n_ct

    first_row = (my_rt * n_ct + my_ct) * src
    which = first_row // child_rows
    first_within = first_row - which * child_rows
    cmap = lax.dynamic_index_in_dim(column_map, which, 0, keepdims=False)
    stairs = lax.dynamic_index_in_dim(staircase, which, 0, keepdims=False)
    limits = jnp.broadcast_to(stairs[:, None], (stairs.shape[0], tile_cols)).reshape(-1)

    edges = STEP * jnp.arange(FRONT_COLS // STEP, dtype=jnp.int32)
    starts = jnp.sum((cmap[None, :] < edges[:, None]).astype(jnp.int32), axis=1)
    starts = jnp.minimum(starts // LANES, (child_cols - STEP - LANES) // LANES)
    info = jnp.concatenate([starts, my_ct[None], first_within[None]]).astype(jnp.int32)
    two, eight = n_ct // 2, n_ct // 8
    near = list(range(1, two))
    near = [near[: -2 * eight], near[-2 * eight : -eight], near[-eight:]]
    far = [list(range(two + k * eight, two + (k + 1) * eight)) for k in range(4)]
    order = [0] + near[0] + near[1] + far[0] + near[2] + far[1] + far[2] + far[3]
    spread = functools.partial(widen, info, children, cmap[None, :], limits[None, :], n_ct=n_ct)
    blocks, mark = spread([0] + near[0] + far[0], tokens=[])

    within = first_within + jnp.arange(src, dtype=jnp.int32)
    panel = jnp.where(within[:, None] < limits[None, :PANEL], children[:, :PANEL], 0.0)
    ct_bits, rt_bits = bits_down(n_ct, 1), bits_down(n_rt, 2)
    steps = [(0, bit) for bit in ct_bits[:-1]] + [(bit, 0) for bit in rt_bits[:-1]]

    rt_order = combos(rt_bits)
    rt_order = rt_order + [r ^ 1 for r in rt_order]
    sources = (my_rt ^ np.array(rt_order, np.int32))[None, :] * n_ct + (
        my_ct ^ np.array(order, np.int32)
    )[:, None]
    targets = row_map.reshape(n_dev, src)[sources.reshape(-1)] - my_rt * front_rows
    targets = targets.reshape(n_ct, 1, n_rt * src)
    flat_targets = targets.reshape(1, total_rows)

    arrived = {0: blocks[0]}

    def over_ct(group, tokens):
        for d, x in zip(group, gate([blocks[d] for d in group], tokens)):
            arrived[d] = swap(x, 0, d)
        return [arrived[d] for d in group]

    def over_rt(bundle, tokens):
        parts = [arrived[d] for d in bundle]
        mine = [join(parts, tokens)[0]] if len(parts) > 1 else list(gate(parts, tokens))
        for bit in rt_bits:
            mine = mine + [swap(x, bit, 0) for x in mine]
        return mine

    for n, (rt_bit, ct_bit) in enumerate(steps):
        last = n == len(steps) - 1
        parts = [panel, swap(panel, rt_bit, ct_bit)]
        panel, mark = join(parts, [mark] if n == 0 else done if last else [], 2 if last else 1)
        if n == 0:
            over_ct(far[0], [mark])
            done = over_ct(near[0], [mark])
            own = over_rt([0], [mark])
            more, after = spread(near[1] + near[2] + far[1] + far[2] + far[3], tokens=[mark])
            blocks |= more
            done = done + own[1:] + [after]
    left, right = panel
    over_ct(near[1], [mark])
    left, mark = join([left, swap(left, rt_bits[-1], 0)], [arrived[d] for d in far[0]])
    right, after = join([right, swap(right, 0, ct_bits[-1])])
    over_ct(far[1], [mark, after])
    left_other, right_other = swap(left, 0, ct_bits[-1]), swap(right, rt_bits[-1], 0)
    panel, gram, mark = gram_of(
        left, left_other, right, right_other, [arrived[d] for d in near[1]]
    )
    other_gram, other_panel = swap(gram, 1, 0), swap(panel, 1, 0)
    over_ct(far[2], [mark])
    over_ct(near[2], [mark])
    first = over_rt(near[0] + near[1] + far[0], [mark])
    inverse, mark = inverse_factor(gram, other_gram, [first[0], other_panel])
    joined_first, mark = join(
        own + first, [mark] + [arrived[d] for d in near[2] + far[1] + far[2]]
    )
    other_first = swap(joined_first, 1, 0)
    over_ct(far[3], [mark])
    second = over_rt(near[2] + far[1], [mark])
    inverse = [inverse]
    half = n_rt // 2
    q_high, q_low, basis, turned_high, turned_low = basis_rows(
        inverse,
        panel.reshape(2, half, n_ct // 2, src, PANEL),
        other_panel.reshape(2, half, n_ct // 2, src, PANEL),
        targets,
        second[:1] + [mark],
        front_rows,
        order,
    )

    size, rest = src * half, first[0].shape[0]
    first_spots = [(side, n * src) for side in range(2) for n in range(half)]
    first_spots += [
        (side, size + n * rest + k * src)
        for k in range(rest // src)
        for side in range(2)
        for n in range(half)
    ]

    def pair_spots(joined, count):
        height = joined.shape[0] // half
        return tuple(
            (side, n * height + k * src) for k in range(count) for side in range(2) for n in range(half)
        )

    call = functools.partial(mix_call, q_high=q_high, q_low=q_low, targets=flat_targets, src=src, front_rows=front_rows)
    waited = list(gate([arrived[d] for d in far[3]] + second[1:], [basis]))
    for d in far[3]:
        arrived[d] = waited.pop(0)
    joined_second, mark = join(second[:1] + waited)
    other_second = swap(joined_second, 1, 0)
    third, fourth = over_rt(far[2], [mark]), over_rt(far[3], [mark])
    state = call(
        first_kernel,
        0,
        (),
        (),
        (joined_first, other_first),
        tuple(first_spots),
        tokens=[third[0], fourth[0], mark],
    )
    waited = list(gate([other_second] + third[1:], [state[0]]))
    other_second, third = waited[0], third[:1] + waited[1:]
    joined_third, mark = join(third + fourth[:1])
    other_third = swap(joined_third, 1, 0)
    state = call(
        more_kernel,
        2,
        tuple(state),
        (),
        (joined_second, other_second),
        pair_spots(joined_second, 2 * eight),
        tokens=[mark],
    )
    fourth = list(gate(fourth[1:], [state[0]]))
    mine = [joined_third] + fourth
    arrays = tuple(mine + [other_third] + [swap(x, 1, 0) for x in fourth])
    height = eight * src
    spots = [
        (side * len(mine), n * height + k * src)
        for k in range(eight)
        for side in range(2)
        for n in range(half)
    ]
    spots += [
        (side * len(mine) + n, (half * height if n == 0 else 0) + k * src)
        for k in range(eight)
        for side in range(2)
        for n in range(half)
    ]
    factor, remainder = call(
        last_kernel, 3, tuple(state), (turned_high, turned_low), arrays, tuple(spots), tokens=[]
    )
    return factor, basis, remainder


def solution(mesh):
    placed = (P(("rt", "ct"), None), P(), P(), P())
    return jax.shard_map(
        shards,
        mesh=mesh,
        in_specs=placed,
        out_specs=(P(None, "ct"), P(None, "rt"), P("rt", "ct")),
        check_vma=False,
    )
```

```python
import functools

import jax
import jax.numpy as jnp
import numpy as np
from jax import lax
from jax.experimental import pallas as pl
from jax.experimental.pallas import tpu as pltpu
from jax.sharding import PartitionSpec as P

FRONT_COLS = 16384
PANEL = 512
STEP = 256
WIDE = 512
LANES = 128
NB = 128
SUB = 8

HI = lax.Precision.HIGHEST
F32 = jnp.float32
BF16 = jnp.bfloat16
MIB = 2**20


def swap(x, rt_bit, ct_bit):
    n_rt, n_ct = lax.axis_size("rt"), lax.axis_size("ct")
    if not rt_bit:
        return lax.ppermute(x, "ct", [(c, c ^ ct_bit) for c in range(n_ct)])
    if not ct_bit:
        return lax.ppermute(x, "rt", [(r, r ^ rt_bit) for r in range(n_rt)])
    pairs = [
        (r * n_ct + c, (r ^ rt_bit) * n_ct + (c ^ ct_bit)) for r in range(n_rt) for c in range(n_ct)
    ]
    return lax.ppermute(x, ("rt", "ct"), pairs)


def bits_down(size, last):
    bit, bits = size // 2, []
    while bit >= last:
        bits.append(bit)
        bit //= 2
    return bits


def combos(bits):
    order = [0]
    for bit in bits:
        order = order + [value ^ bit for value in order]
    return order


def halves(x):
    high = x.astype(BF16)
    return high, (x - high.astype(F32)).astype(BF16)


def dot(a, b):
    return jnp.dot(a, b, preferred_element_type=F32)


def dot_nt(a, b, precision=None):
    return lax.dot_general(
        a, b, (((1,), (1,)), ((), ())), precision=precision, preferred_element_type=F32
    )


def dot_tn(a, b, precision=None):
    return lax.dot_general(
        a, b, (((0,), (0,)), ((), ())), precision=precision, preferred_element_type=F32
    )


MARK = jax.ShapeDtypeStruct((SUB, LANES), F32)


def params(mib):
    return pltpu.CompilerParams(vmem_limit_bytes=mib * MIB)


def widen_kernel(tiles, window, places, waits, info, child, cmap, limits, *outs):
    rows = child.shape[0]
    my_block = info[info.shape[0] - 2]
    first_row = info[info.shape[0] - 1]
    row_ids = first_row + lax.broadcasted_iota(jnp.int32, (rows, window), 0)
    col_ids = lax.broadcasted_iota(jnp.int32, (STEP, window), 0)
    made = iter(outs[waits:-1])
    for place, cut in places:
        block = my_block ^ place
        parts = [next(made) for _ in range(cut)]

        def tile(i, carry, block=block, parts=parts):
            t = block * tiles + i
            cols = pl.ds(pl.multiple_of(info[t] * LANES, LANES), window)
            live = jnp.where(row_ids < limits[:, cols], child[:, cols], 0.0)
            hot = jnp.where(col_ids == cmap[:, cols] - t * STEP, 1.0, 0.0).astype(BF16)
            spread = dot_nt(jnp.concatenate(halves(live), axis=0), hot)
            spread = spread[:rows] + spread[rows:]
            there = pl.ds(pl.multiple_of(i * STEP, STEP), STEP)
            height = rows // len(parts)
            for k, part in enumerate(parts):
                part[:, there] = spread[k * height : (k + 1) * height]
            return carry

        lax.fori_loop(0, tiles, tile, 0, unroll=4)


def widen(info, child, cmap, limits, places, n_ct, tokens):
    rows, width = child.shape
    block_cols = FRONT_COLS // n_ct
    window = STEP + LANES
    whole = pl.BlockSpec(memory_space=pltpu.VMEM)
    made = pl.pallas_call(
        functools.partial(widen_kernel, block_cols // STEP, window, tuple(places), len(tokens)),
        out_shape=[
            jax.ShapeDtypeStruct((rows // cut, block_cols), F32)
            for _, cut in places
            for _ in range(cut)
        ]
        + [MARK],
        in_specs=[pl.BlockSpec(memory_space=pltpu.SMEM), whole, whole, whole]
        + [pl.BlockSpec(memory_space=pl.ANY)] * len(tokens),
        out_specs=[whole] * sum(cut for _, cut in places) + [pl.BlockSpec(memory_space=pl.ANY)],
        compiler_params=params(63),
        cost_estimate=pl.CostEstimate(
            flops=4 * rows * window * block_cols * len(places),
            bytes_accessed=4 * rows * (width + block_cols * len(places)),
            transcendentals=0,
        ),
    )(info, child, cmap, limits, *tokens)
    keys = [(d, k) for d, cut in places for k in range(cut)]
    return dict(zip(keys, made)), made[-1]


def small_inverse(tile):
    a = [
        [jnp.broadcast_to(tile[i : i + 1, k : k + 1], (SUB, NB)) for k in range(i + 1)]
        for i in range(SUB)
    ]
    scale = [None] * SUB
    lower = [[None] * SUB for _ in range(SUB)]
    inverse = [[None] * SUB for _ in range(SUB)]
    for j in range(SUB):
        scale[j] = lax.rsqrt(a[j][j])
        for i in range(j + 1, SUB):
            lower[i][j] = a[i][j] * scale[j]
        for i in range(j + 1, SUB):
            for k in range(j + 1, i + 1):
                a[i][k] = a[i][k] - lower[i][j] * lower[k][j]
    for j in range(SUB):
        inverse[j][j] = scale[j]
        for i in range(j + 1, SUB):
            total = lower[i][j] * inverse[j][j]
            for k in range(j + 1, i):
                total = total + lower[i][k] * inverse[k][j]
            inverse[i][j] = -scale[i] * total
    return inverse


def apply_small(inverse, tiles):
    sub = lax.broadcasted_iota(jnp.int32, (SUB, NB), 0)
    outs = [None] * len(tiles)
    for k in range(SUB):
        column = jnp.zeros((SUB, NB), F32)
        for i in range(k, SUB):
            column = jnp.where(sub == i, inverse[i][k], column)
        for n, tile in enumerate(tiles):
            term = column * jnp.broadcast_to(tile[k : k + 1, :], (SUB, NB))
            outs[n] = term if outs[n] is None else outs[n] + term
    return outs


def identity(n):
    shape = (n, n)
    same = lax.broadcasted_iota(jnp.int32, shape, 0) == lax.broadcasted_iota(jnp.int32, shape, 1)
    return jnp.where(same, 1.0, 0.0)


def thirds(x):
    high = x.astype(BF16)
    rest = x - high.astype(F32)
    mid = rest.astype(BF16)
    return high, mid, (rest - mid.astype(F32)).astype(BF16)


def diagonal_inverse(block, out, work):
    lane = lax.broadcasted_iota(jnp.int32, (SUB, NB), 1)
    work[:NB, :NB] = block
    work[:NB, NB:] = identity(NB)
    work[NB:, :] = jnp.zeros((SUB, 2 * NB), F32)

    def body(s, carry):
        tile, before = carry
        h, m, l = thirds(before)
        left = jnp.concatenate([x[:, :NB] for x in (h, h, m, h, l, m)], axis=0)
        right = jnp.concatenate([h, m, h, l, h, m], axis=0)
        work[:NB, :] = work[:NB, :] - dot_tn(left, right)
        after = work[pl.ds(pl.multiple_of(SUB * s + SUB, SUB), SUB), :]
        shift = lax.rem(NB - SUB * s, NB)
        inverse = small_inverse(pltpu.roll(tile[:, :NB], shift, 1))
        turned = pltpu.roll(after[:, :NB], shift, 1)
        top, top_right = apply_small(inverse, [tile[:, :NB], tile[:, NB:]])
        out[pl.ds(pl.multiple_of(SUB * s, SUB), SUB), :] = top_right
        top = jnp.concatenate([jnp.where(lane >= SUB * s, top, 0.0), top_right], axis=1)
        columns = [jnp.broadcast_to(turned[:, k : k + 1], (SUB, NB)) for k in range(SUB)]
        for i in range(SUB):
            weight = inverse[i][0] * columns[0]
            for k in range(1, i + 1):
                weight = weight + inverse[i][k] * columns[k]
            weight = jnp.concatenate([weight, weight], axis=1)
            after = after - weight * jnp.broadcast_to(top[i : i + 1], (SUB, 2 * NB))
        return after, top

    lax.fori_loop(0, NB // SUB, body, (work[:SUB, :], jnp.zeros((SUB, 2 * NB), F32)))


def factor_kernel(gram_a, gram_b, *refs):
    out, _, whole, small, work = refs[-5:]
    n = out.shape[0]
    whole[:, :n] = gram_a[...] + gram_b[...]
    whole[:, n:] = identity(n)
    for lo in range(0, n, NB):
        hi = lo + NB
        diagonal_inverse(whole[lo:hi, lo:hi], small, work)
        rows = jnp.dot(small[...], whole[lo:hi, lo : n + hi], precision=HI, preferred_element_type=F32)
        out[lo:hi, :hi] = rows[:, n - lo :]
        if hi < n:
            out[lo:hi, hi:] = jnp.zeros((NB, n - hi), F32)
            whole[hi:, hi : n + hi] -= dot_tn(rows[:, NB : n - lo], rows[:, NB:], HI)


def inverse_factor(gram_a, gram_b, tokens):
    n = gram_a.shape[0]
    whole = pl.BlockSpec(memory_space=pltpu.VMEM)
    return pl.pallas_call(
        factor_kernel,
        out_shape=[jax.ShapeDtypeStruct((n, n), F32), MARK],
        in_specs=[whole] * 2 + [pl.BlockSpec(memory_space=pl.ANY)] * len(tokens),
        out_specs=[whole, pl.BlockSpec(memory_space=pl.ANY)],
        scratch_shapes=[
            pltpu.VMEM((n, 2 * n), F32),
            pltpu.VMEM((NB, NB), F32),
            pltpu.VMEM((NB + SUB, 2 * NB), F32),
        ],
        compiler_params=params(63),
        cost_estimate=pl.CostEstimate(
            flops=30 * 10**9, bytes_accessed=12 * n * n, transcendentals=0
        ),
    )(gram_a, gram_b, *tokens)


def gate_kernel(*refs):
    pass


def gate(arrays, tokens):
    if not arrays:
        return []
    anywhere = pl.BlockSpec(memory_space=pl.ANY)
    return pl.pallas_call(
        gate_kernel,
        out_shape=[jax.ShapeDtypeStruct(x.shape, x.dtype) for x in arrays],
        in_specs=[anywhere] * (len(arrays) + len(tokens)),
        out_specs=[anywhere] * len(arrays),
        input_output_aliases={k: k for k in range(len(arrays))},
        cost_estimate=pl.CostEstimate(flops=0, bytes_accessed=0, transcendentals=0),
    )(*arrays, *tokens)


def join_kernel(count, cut, *refs):
    parts, outs = refs[:count], refs[-cut - 1 : -1]
    width = outs[0].shape[1]
    row = 0
    for part in parts:
        rows = part.shape[0]
        for k, out in enumerate(outs):
            out[row : row + rows, :] = part[:, k * width : (k + 1) * width]
        row += rows


def join(parts, tokens=(), cut=1):
    rows, width = sum(x.shape[0] for x in parts), parts[0].shape[1]
    whole = pl.BlockSpec(memory_space=pltpu.VMEM)
    out = pl.pallas_call(
        functools.partial(join_kernel, len(parts), cut),
        out_shape=[jax.ShapeDtypeStruct((rows, width // cut), F32)] * cut + [MARK],
        in_specs=[whole] * len(parts) + [pl.BlockSpec(memory_space=pl.ANY)] * len(tokens),
        out_specs=[whole] * cut + [pl.BlockSpec(memory_space=pl.ANY)],
        compiler_params=params(16 if width <= PANEL else 63),
        cost_estimate=pl.CostEstimate(
            flops=0, bytes_accessed=8 * rows * width, transcendentals=0
        ),
    )(*parts, *tokens)
    return (out[:cut] if cut > 1 else out[0]), out[-1]


def gram_kernel(a_mine, a_other, b_mine, b_other, *refs):
    panel, gram = refs[-3:-1]
    half, width = a_mine.shape
    quarter = half // 2
    panel[:half, :width] = a_mine[...]
    panel[half:, :width] = a_other[...]
    for k, source in enumerate((b_mine, b_other)):
        panel[k * quarter : (k + 1) * quarter, width:] = source[:quarter, :]
        panel[half + k * quarter : half + (k + 1) * quarter, width:] = source[quarter:, :]
    rows = panel[...]
    gram[...] = dot_tn(rows, rows, HI)


def gram_of(a_mine, a_other, b_mine, b_other, tokens):
    half, width = a_mine.shape
    whole = pl.BlockSpec(memory_space=pltpu.VMEM)
    return pl.pallas_call(
        gram_kernel,
        out_shape=[
            jax.ShapeDtypeStruct((2 * half, 2 * width), F32),
            jax.ShapeDtypeStruct((2 * width, 2 * width), F32),
            MARK,
        ],
        in_specs=[whole] * 4 + [pl.BlockSpec(memory_space=pl.ANY)] * len(tokens),
        out_specs=[whole] * 2 + [pl.BlockSpec(memory_space=pl.ANY)],
        compiler_params=params(24),
        cost_estimate=pl.CostEstimate(
            flops=4 * half * 4 * width * width, bytes_accessed=4 * half * width, transcendentals=0
        ),
    )(a_mine, a_other, b_mine, b_other, *tokens)


def basis_kernel(count, waits, *refs):
    inverse, refs = refs[:count], refs[count:]
    own, other, targets = refs[:3]
    q_high, q_low, basis, turned_high, turned_low = refs[3 + waits :]
    d = pl.program_id(0)
    group, panel = targets.shape[-1], inverse[0].shape[1]
    rows = jnp.concatenate(
        [own[...].reshape(group // 2, panel), other[...].reshape(group // 2, panel)], axis=0
    )
    inv_high, inv_low = halves(inverse[0][...])
    high, low = halves(rows)
    q = dot_nt(inv_high, high) + (dot_nt(inv_low, high) + dot_nt(inv_high, low))
    q_h, q_l = halves(q)
    q_high[...] = q_h
    q_low[...] = q_l
    front = basis.shape[1]
    ids = lax.broadcasted_iota(jnp.int32, (front, group), 0)
    hot = jnp.where(ids == targets[0], 1.0, 0.0).astype(BF16)
    part = dot_nt(q_h, hot) + dot_nt(q_l, hot)

    @pl.when(d == 0)
    def _():
        basis[...] = part

    @pl.when(d > 0)
    def _():
        basis[...] += part

    @pl.when(d == pl.num_programs(0) - 1)
    def _():
        turned_h, turned_l = halves(basis[...].T)
        turned_high[...] = turned_h
        turned_low[...] = turned_l


def basis_rows(inverse, own, other, targets, tokens, front_rows, order):
    last, half, upper, src, panel = own.shape
    n_ct = last * upper
    group = 2 * half * src
    depth = upper.bit_length() - 1

    def place(step):
        d = sum(jnp.where(step == k, value, 0) for k, value in enumerate(order))
        spot = sum(((d >> (k + 1)) & 1) << (depth - 1 - k) for k in range(depth))
        return (d & 1, 0, spot, 0, 0)

    wide = jax.ShapeDtypeStruct((panel, n_ct * group), BF16)
    return pl.pallas_call(
        functools.partial(basis_kernel, len(inverse), len(tokens)),
        grid=(n_ct,),
        out_shape=[
            wide,
            wide,
            jax.ShapeDtypeStruct((panel, front_rows), F32),
            jax.ShapeDtypeStruct((front_rows, panel), BF16),
            jax.ShapeDtypeStruct((front_rows, panel), BF16),
        ],
        in_specs=[
            *[pl.BlockSpec((panel, panel), lambda d: (0, 0)) for _ in inverse],
            pl.BlockSpec((1, half, 1, src, panel), place),
            pl.BlockSpec((1, half, 1, src, panel), place),
            pl.BlockSpec((1, 1, group), lambda d: (d, 0, 0)),
            *[pl.BlockSpec(memory_space=pl.ANY) for _ in tokens],
        ],
        out_specs=[
            pl.BlockSpec((panel, group), lambda d: (0, d)),
            pl.BlockSpec((panel, group), lambda d: (0, d)),
            pl.BlockSpec((panel, front_rows), lambda d: (0, 0)),
            pl.BlockSpec((front_rows, panel), lambda d: (0, 0)),
            pl.BlockSpec((front_rows, panel), lambda d: (0, 0)),
        ],
        compiler_params=params(63),
        cost_estimate=pl.CostEstimate(
            flops=8 * panel * panel * n_ct * group, bytes_accessed=6 * MIB, transcendentals=0
        ),
    )(*inverse, own, other, targets, *tokens)


def mix(q_high, q_low, hot, pieces, spots):
    rows = jnp.concatenate([pieces[n][lo : lo + size, :] for n, lo, size in spots], axis=0)
    high, low = halves(rows)
    factor = dot(q_high[...], high) + (dot(q_low[...], high) + dot(q_high[...], low))
    return factor, dot(hot[...], high) + dot(hot[...], low)


def build_hot(targets, hot):
    @pl.when(pl.program_id(0) == 0)
    def _():
        ids = lax.broadcasted_iota(jnp.int32, hot.shape, 0)
        hot[...] = jnp.where(ids == targets[...], 1.0, 0.0).astype(BF16)


def first_kernel(count, spots, q_high, q_low, targets, *refs):
    pieces, (factor, placed, hot) = refs[:count], refs[-3:]
    build_hot(targets, hot)
    factor[...], placed[...] = mix(q_high, q_low, hot, pieces, spots)


def more_kernel(count, spots, q_high, q_low, targets, factor_in, placed_in, *refs):
    pieces, (factor, placed, hot) = refs[:count], refs[-3:]
    build_hot(targets, hot)
    add_factor, add_placed = mix(q_high, q_low, hot, pieces, spots)
    factor[...] = factor_in[...] + add_factor
    placed[...] = placed_in[...] + add_placed


def last_kernel(count, spots, q_high, q_low, targets, factor_in, placed_in, turned_high, turned_low, *refs):
    pieces, (factor, remainder, hot) = refs[:count], refs[-3:]
    build_hot(targets, hot)
    add_factor, add_placed = mix(q_high, q_low, hot, pieces, spots)
    total = factor_in[...] + add_factor
    factor[...] = total
    high, low = halves(total)
    removed = dot(turned_high[...], high) + (dot(turned_low[...], high) + dot(turned_high[...], low))
    remainder[...] = (placed_in[...] + add_placed) - removed


def mix_call(kernel, group, extra, turned, pieces, spots, q_high, q_low, targets, front_rows, tokens):
    panel = q_high.shape[0]
    block_cols = pieces[0].shape[1]
    depth = sum(size for _, _, size in spots)
    column = lambda j: (0, j)
    fixed = lambda j: (0, group)
    still = lambda j: (0, 0)
    flops = depth * block_cols * (3 * panel + 2 * front_rows)
    flops += 3 * panel * front_rows * block_cols if turned else 0
    return pl.pallas_call(
        functools.partial(kernel, len(pieces), spots),
        grid=(block_cols // WIDE,),
        out_shape=[
            jax.ShapeDtypeStruct((panel, block_cols), F32),
            jax.ShapeDtypeStruct((front_rows, block_cols), F32),
        ],
        in_specs=[
            pl.BlockSpec((panel, depth), fixed),
            pl.BlockSpec((panel, depth), fixed),
            pl.BlockSpec((1, depth), fixed),
        ]
        + [pl.BlockSpec((x.shape[0], WIDE), column) for x in extra]
        + [pl.BlockSpec(x.shape, still) for x in turned]
        + [pl.BlockSpec((x.shape[0], WIDE), column) for x in pieces]
        + [pl.BlockSpec(memory_space=pl.ANY)] * len(tokens),
        out_specs=[
            pl.BlockSpec((panel, WIDE), column),
            pl.BlockSpec((front_rows, WIDE), column),
        ],
        scratch_shapes=[pltpu.VMEM((front_rows, depth), BF16)],
        compiler_params=params(63),
        cost_estimate=pl.CostEstimate(
            flops=flops,
            bytes_accessed=block_cols * (depth + (1 + bool(extra)) * (panel + front_rows)),
            transcendentals=0,
        ),
    )(q_high, q_low, targets, *extra, *turned, *pieces, *tokens)


def shards(children, row_map, column_map, staircase):
    n_rt, n_ct = lax.axis_size("rt"), lax.axis_size("ct")
    my_rt, my_ct = lax.axis_index("rt"), lax.axis_index("ct")
    src, child_cols = children.shape
    total_rows = row_map.shape[0]
    child_rows = total_rows // 2
    front_rows = total_rows // n_rt
    tile_cols = child_cols // staircase.shape[1]
    n_dev = n_rt * n_ct

    first_row = (my_rt * n_ct + my_ct) * src
    which = first_row // child_rows
    first_within = first_row - which * child_rows
    cmap = lax.dynamic_index_in_dim(column_map, which, 0, keepdims=False)
    stairs = lax.dynamic_index_in_dim(staircase, which, 0, keepdims=False)
    limits = jnp.broadcast_to(stairs[:, None], (stairs.shape[0], tile_cols)).reshape(-1)

    edges = STEP * jnp.arange(FRONT_COLS // STEP, dtype=jnp.int32)
    starts = jnp.sum((cmap[None, :] < edges[:, None]).astype(jnp.int32), axis=1)
    starts = jnp.minimum(starts // LANES, (child_cols - STEP - LANES) // LANES)
    info = jnp.concatenate([starts, my_ct[None], first_within[None]]).astype(jnp.int32)
    two, eight = n_ct // 2, n_ct // 8
    near = sorted(range(1, two), key=lambda d: d % 2)
    near = [near[: -2 * eight], near[-2 * eight : -eight], near[-eight:]]
    far = [list(range(two + k * eight, two + (k + 1) * eight)) for k in range(4)]
    order = [0] + near[0] + far[0] + near[1] + far[1] + near[2] + far[2] + far[3]
    spread = functools.partial(widen, info, children, cmap[None, :], limits[None, :], n_ct=n_ct)
    ones = lambda groups: [(d, 1) for group in groups for d in group]
    blocks, mark = spread(ones([near[0]]), tokens=[])

    within = first_within + jnp.arange(src, dtype=jnp.int32)
    panel = jnp.where(within[:, None] < limits[None, :PANEL], children[:, :PANEL], 0.0)
    ct_bits, rt_bits = bits_down(n_ct, 1), bits_down(n_rt, 2)

    rt_order = combos(rt_bits)
    rt_order = rt_order + [r ^ 1 for r in rt_order]
    sources = (my_rt ^ np.array(rt_order, np.int32))[None, :] * n_ct + (
        my_ct ^ np.array(order, np.int32)
    )[:, None]
    targets = row_map.reshape(n_dev, src)[sources.reshape(-1)] - my_rt * front_rows
    targets = targets.reshape(n_ct, 1, n_rt * src)
    flat_targets = targets.reshape(1, total_rows)

    half = n_rt // 2

    def over_ct(group, tokens, part=0):
        operands = gate([blocks[d, part] for d in group], tokens)
        return [swap(x, 0, d) for d, x in zip(group, operands)]

    def over_rt(mine):
        mine = [mine]
        for bit in rt_bits:
            mine = mine + [swap(x, bit, 0) for x in mine]
        return mine

    def one(arrays):
        return arrays[0] if len(arrays) == 1 else join(arrays)[0]

    parts = [panel] + [swap(panel, 0, bits) for bits in combos(ct_bits[:-1])[1:]]
    for bit in rt_bits[:-1]:
        panel, _ = join(parts)
        parts = [panel, swap(panel, bit, 0)]
    (left, right), mark = join(parts, [mark], cut=2)
    near_a = over_ct(near[0], [mark])
    later = ones([[0]] + near[1:] + far[1:]) + [(d, 2) for d in far[0]]
    more, after = spread(later, tokens=[mark])
    blocks |= more
    left, mark = join([left, swap(left, rt_bits[-1], 0)], [after])
    right, _ = join([right, swap(right, 0, ct_bits[-1])])
    far_a = over_ct(far[0], [mark])
    left_other, right_other = swap(left, 0, ct_bits[-1]), swap(right, rt_bits[-1], 0)
    panel, gram, mark = gram_of(left, left_other, right, right_other, near_a + far_a)
    other_gram, other_panel = swap(gram, 1, 0), swap(panel, 1, 0)
    far_e = over_ct(far[0], [mark], 1)
    far_b, near_b = over_ct(far[1], [mark]), over_ct(near[1], [mark])
    joined, after = join([blocks[0, 0]] + near_a + far_a, [mark])
    first = over_rt(joined)
    inverse, mark = inverse_factor(gram, other_gram, [other_panel, after])

    late = list(gate(first + near_b + far_e + far_b, [mark]))
    first, late = late[:half], late[half:]
    far_c, near_c = over_ct(far[2], late[:1]), over_ct(near[2], late[:1])
    joined, mark = join(late[eight : 2 * eight] + late[:eight] + late[2 * eight :])
    second = over_rt(joined)
    first, after = join(first)
    first = [first, swap(first, 1, 0)]
    inverse = [inverse]
    q_high, q_low, basis, turned_high, turned_low = basis_rows(
        inverse,
        panel.reshape(2, half, n_ct // 2, src, PANEL),
        other_panel.reshape(2, half, n_ct // 2, src, PANEL),
        targets,
        [mark, after],
        front_rows,
        order,
    )

    call = functools.partial(mix_call, q_high=q_high, q_low=q_low, targets=flat_targets, front_rows=front_rows)
    late = list(gate(second + near_c + far_c, [basis]))
    second, late = late[:half], late[half:]
    far_d = over_ct(far[3], late[:1])
    third, fourth = over_rt(one(late[:eight])), over_rt(one(late[eight:]))
    second += [swap(x, 1, 0) for x in second]

    def rows_of(mine, start, size):
        return [(mine + n, start, size) for n in range(n_rt)]

    def group(bundles):
        arrays, spots = [], []
        for mine in bundles:
            for row in range(0, mine[0].shape[0], src):
                spots += rows_of(len(arrays), row, src)
            arrays += mine
        return tuple(arrays), tuple(spots)

    part, height = src // 2, first[0].shape[0] // half
    whole_rows = height - part * eight
    places = [(side, n * height) for side in range(2) for n in range(half)]
    spots = [(side, at + row, src) for row in range(0, whole_rows, src) for side, at in places]
    for k in range(eight):
        for n, (side, at) in enumerate(places):
            spots += [(side, at + whole_rows + k * part, part), (2 + n, k * part, part)]
    for row in range(part * eight, second[0].shape[0], src):
        spots += rows_of(2, row, src)
    arrays = tuple(first) + tuple(second)
    state = call(first_kernel, 0, (), (), arrays, tuple(spots), tokens=late[:1])
    late = list(gate(third + fourth + far_d, [state[0]]))
    third, fourth, late = late[:half], late[half : 2 * half], late[2 * half :]
    fifth = over_rt(one(late))
    third += [swap(x, 1, 0) for x in third]
    fourth += [swap(x, 1, 0) for x in fourth]
    state = call(more_kernel, 5, tuple(state), (), *group((third,)), tokens=fourth[half:])
    fifth = list(gate(fifth, [state[0]]))
    fifth += [swap(x, 1, 0) for x in fifth]
    turned = (turned_high, turned_low)
    factor, remainder = call(last_kernel, 3, tuple(state), turned, *group((fourth, fifth)), tokens=[])
    return factor, basis, remainder


def solution(mesh):
    placed = (P(("rt", "ct"), None), P(), P(), P())
    return jax.shard_map(
        shards,
        mesh=mesh,
        in_specs=placed,
        out_specs=(P(None, "ct"), P(None, "rt"), P("rt", "ct")),
        check_vma=False,
    )
```

```python
import functools

import jax
import jax.numpy as jnp
import numpy as np
from jax import lax
from jax.experimental import pallas as pl
from jax.experimental.pallas import tpu as pltpu
from jax.sharding import PartitionSpec as P

FRONT_COLS = 16384
PANEL = 512
STEP = 256
WIDE = 512
UNROLL = 8
LANES = 128
NB = 128
SUB = 8

HI = lax.Precision.HIGHEST
F32 = jnp.float32
BF16 = jnp.bfloat16
MIB = 2**20


def swap(x, rt_bit, ct_bit):
    n_rt, n_ct = lax.axis_size("rt"), lax.axis_size("ct")
    if not rt_bit:
        return lax.ppermute(x, "ct", [(c, c ^ ct_bit) for c in range(n_ct)])
    if not ct_bit:
        return lax.ppermute(x, "rt", [(r, r ^ rt_bit) for r in range(n_rt)])
    pairs = [
        (r * n_ct + c, (r ^ rt_bit) * n_ct + (c ^ ct_bit)) for r in range(n_rt) for c in range(n_ct)
    ]
    return lax.ppermute(x, ("rt", "ct"), pairs)


def bits_down(size, last):
    bit, bits = size // 2, []
    while bit >= last:
        bits.append(bit)
        bit //= 2
    return bits


def combos(bits):
    order = [0]
    for bit in bits:
        order = order + [value ^ bit for value in order]
    return order


def halves(x):
    high = x.astype(BF16)
    return high, (x - high.astype(F32)).astype(BF16)


def dot(a, b):
    return jnp.dot(a, b, preferred_element_type=F32)


def dot_nt(a, b, precision=None):
    return lax.dot_general(
        a, b, (((1,), (1,)), ((), ())), precision=precision, preferred_element_type=F32
    )


def dot_tn(a, b, precision=None):
    return lax.dot_general(
        a, b, (((0,), (0,)), ((), ())), precision=precision, preferred_element_type=F32
    )


MARK = jax.ShapeDtypeStruct((SUB, LANES), F32)


def params(mib):
    return pltpu.CompilerParams(vmem_limit_bytes=mib * MIB)


def widen_kernel(tiles, window, places, waits, info, child, cmap, limits, *outs):
    rows = child.shape[0]
    my_block = info[info.shape[0] - 2]
    first_row = info[info.shape[0] - 1]
    row_ids = first_row + lax.broadcasted_iota(jnp.int32, (rows, window), 0)
    col_ids = lax.broadcasted_iota(jnp.int32, (STEP, window), 0)
    made = iter(outs[waits:-1])
    for place, cut in places:
        block = my_block ^ place
        parts = [next(made) for _ in range(cut)]

        def tile(i, carry, block=block, parts=parts):
            t = block * tiles + i
            cols = pl.ds(pl.multiple_of(info[t] * LANES, LANES), window)
            live = jnp.where(row_ids < limits[:, cols], child[:, cols], 0.0)
            hot = jnp.where(col_ids == cmap[:, cols] - t * STEP, 1.0, 0.0).astype(BF16)
            spread = dot_nt(jnp.concatenate(halves(live), axis=0), hot)
            spread = spread[:rows] + spread[rows:]
            there = pl.ds(pl.multiple_of(i * STEP, STEP), STEP)
            height = rows // len(parts)
            for k, part in enumerate(parts):
                part[:, there] = spread[k * height : (k + 1) * height]
            return carry

        lax.fori_loop(0, tiles, tile, 0, unroll=UNROLL)


def widen(info, child, cmap, limits, places, n_ct, tokens):
    rows, width = child.shape
    block_cols = FRONT_COLS // n_ct
    window = STEP + LANES
    whole = pl.BlockSpec(memory_space=pltpu.VMEM)
    made = pl.pallas_call(
        functools.partial(widen_kernel, block_cols // STEP, window, tuple(places), len(tokens)),
        out_shape=[
            jax.ShapeDtypeStruct((rows // cut, block_cols), F32)
            for _, cut in places
            for _ in range(cut)
        ]
        + [MARK],
        in_specs=[pl.BlockSpec(memory_space=pltpu.SMEM), whole, whole, whole]
        + [pl.BlockSpec(memory_space=pl.ANY)] * len(tokens),
        out_specs=[whole] * sum(cut for _, cut in places) + [pl.BlockSpec(memory_space=pl.ANY)],
        compiler_params=params(63),
        cost_estimate=pl.CostEstimate(
            flops=4 * rows * window * block_cols * len(places),
            bytes_accessed=4 * rows * (width + block_cols * len(places)),
            transcendentals=0,
        ),
    )(info, child, cmap, limits, *tokens)
    keys = [(d, k) for d, cut in places for k in range(cut)]
    return dict(zip(keys, made)), made[-1]


def small_inverse(tile):
    a = [
        [jnp.broadcast_to(tile[i : i + 1, k : k + 1], (SUB, NB)) for k in range(i + 1)]
        for i in range(SUB)
    ]
    scale = [None] * SUB
    lower = [[None] * SUB for _ in range(SUB)]
    inverse = [[None] * SUB for _ in range(SUB)]
    for j in range(SUB):
        scale[j] = lax.rsqrt(a[j][j])
        for i in range(j + 1, SUB):
            lower[i][j] = a[i][j] * scale[j]
        for i in range(j + 1, SUB):
            for k in range(j + 1, i + 1):
                a[i][k] = a[i][k] - lower[i][j] * lower[k][j]
    for j in range(SUB):
        inverse[j][j] = scale[j]
        for i in range(j + 1, SUB):
            total = lower[i][j] * inverse[j][j]
            for k in range(j + 1, i):
                total = total + lower[i][k] * inverse[k][j]
            inverse[i][j] = -scale[i] * total
    return inverse


def apply_small(inverse, tiles):
    sub = lax.broadcasted_iota(jnp.int32, (SUB, NB), 0)
    outs = [None] * len(tiles)
    for k in range(SUB):
        column = jnp.zeros((SUB, NB), F32)
        for i in range(k, SUB):
            column = jnp.where(sub == i, inverse[i][k], column)
        for n, tile in enumerate(tiles):
            term = column * jnp.broadcast_to(tile[k : k + 1, :], (SUB, NB))
            outs[n] = term if outs[n] is None else outs[n] + term
    return outs


def identity(n):
    shape = (n, n)
    same = lax.broadcasted_iota(jnp.int32, shape, 0) == lax.broadcasted_iota(jnp.int32, shape, 1)
    return jnp.where(same, 1.0, 0.0)


def thirds(x):
    high = x.astype(BF16)
    rest = x - high.astype(F32)
    mid = rest.astype(BF16)
    return high, mid, (rest - mid.astype(F32)).astype(BF16)


def diagonal_inverse(block, out, work):
    lane = lax.broadcasted_iota(jnp.int32, (SUB, NB), 1)
    work[:NB, :NB] = block
    work[:NB, NB:] = identity(NB)
    work[NB:, :] = jnp.zeros((SUB, 2 * NB), F32)

    def body(s, carry):
        tile, before = carry
        h, m, l = thirds(before)
        left = jnp.concatenate([x[:, :NB] for x in (h, h, m, h, l, m)], axis=0)
        right = jnp.concatenate([h, m, h, l, h, m], axis=0)
        work[:NB, :] = work[:NB, :] - dot_tn(left, right)
        after = work[pl.ds(pl.multiple_of(SUB * s + SUB, SUB), SUB), :]
        shift = lax.rem(NB - SUB * s, NB)
        inverse = small_inverse(pltpu.roll(tile[:, :NB], shift, 1))
        turned = pltpu.roll(after[:, :NB], shift, 1)
        top, top_right = apply_small(inverse, [tile[:, :NB], tile[:, NB:]])
        out[pl.ds(pl.multiple_of(SUB * s, SUB), SUB), :] = top_right
        top = jnp.concatenate([jnp.where(lane >= SUB * s, top, 0.0), top_right], axis=1)
        columns = [jnp.broadcast_to(turned[:, k : k + 1], (SUB, NB)) for k in range(SUB)]
        for i in range(SUB):
            weight = inverse[i][0] * columns[0]
            for k in range(1, i + 1):
                weight = weight + inverse[i][k] * columns[k]
            weight = jnp.concatenate([weight, weight], axis=1)
            after = after - weight * jnp.broadcast_to(top[i : i + 1], (SUB, 2 * NB))
        return after, top

    lax.fori_loop(0, NB // SUB, body, (work[:SUB, :], jnp.zeros((SUB, 2 * NB), F32)))


def factor_kernel(gram_a, gram_b, *refs):
    out, _, whole, small, work = refs[-5:]
    n = out.shape[0]
    whole[:, :n] = gram_a[...] + gram_b[...]
    whole[:, n:] = identity(n)
    for lo in range(0, n, NB):
        hi = lo + NB
        diagonal_inverse(whole[lo:hi, lo:hi], small, work)
        rows = jnp.dot(small[...], whole[lo:hi, lo : n + hi], precision=HI, preferred_element_type=F32)
        out[lo:hi, :hi] = rows[:, n - lo :]
        if hi < n:
            out[lo:hi, hi:] = jnp.zeros((NB, n - hi), F32)
            whole[hi:, hi : n + hi] -= dot_tn(rows[:, NB : n - lo], rows[:, NB:], HI)


def inverse_factor(gram_a, gram_b, tokens):
    n = gram_a.shape[0]
    whole = pl.BlockSpec(memory_space=pltpu.VMEM)
    return pl.pallas_call(
        factor_kernel,
        out_shape=[jax.ShapeDtypeStruct((n, n), F32), MARK],
        in_specs=[whole] * 2 + [pl.BlockSpec(memory_space=pl.ANY)] * len(tokens),
        out_specs=[whole, pl.BlockSpec(memory_space=pl.ANY)],
        scratch_shapes=[
            pltpu.VMEM((n, 2 * n), F32),
            pltpu.VMEM((NB, NB), F32),
            pltpu.VMEM((NB + SUB, 2 * NB), F32),
        ],
        compiler_params=params(63),
        cost_estimate=pl.CostEstimate(
            flops=30 * 10**9, bytes_accessed=12 * n * n, transcendentals=0
        ),
    )(gram_a, gram_b, *tokens)


def gate_kernel(*refs):
    pass


def gate(arrays, tokens):
    if not arrays:
        return []
    anywhere = pl.BlockSpec(memory_space=pl.ANY)
    return pl.pallas_call(
        gate_kernel,
        out_shape=[jax.ShapeDtypeStruct(x.shape, x.dtype) for x in arrays],
        in_specs=[anywhere] * (len(arrays) + len(tokens)),
        out_specs=[anywhere] * len(arrays),
        input_output_aliases={k: k for k in range(len(arrays))},
        cost_estimate=pl.CostEstimate(flops=0, bytes_accessed=0, transcendentals=0),
    )(*arrays, *tokens)


def join_kernel(count, cut, *refs):
    parts, outs = refs[:count], refs[-cut - 1 : -1]
    width = outs[0].shape[1]
    row = 0
    for part in parts:
        rows = part.shape[0]
        for k, out in enumerate(outs):
            out[row : row + rows, :] = part[:, k * width : (k + 1) * width]
        row += rows


def join(parts, tokens=(), cut=1):
    rows, width = sum(x.shape[0] for x in parts), parts[0].shape[1]
    whole = pl.BlockSpec(memory_space=pltpu.VMEM)
    out = pl.pallas_call(
        functools.partial(join_kernel, len(parts), cut),
        out_shape=[jax.ShapeDtypeStruct((rows, width // cut), F32)] * cut + [MARK],
        in_specs=[whole] * len(parts) + [pl.BlockSpec(memory_space=pl.ANY)] * len(tokens),
        out_specs=[whole] * cut + [pl.BlockSpec(memory_space=pl.ANY)],
        compiler_params=params(16 if width <= PANEL else 63),
        cost_estimate=pl.CostEstimate(
            flops=0, bytes_accessed=8 * rows * width, transcendentals=0
        ),
    )(*parts, *tokens)
    return (out[:cut] if cut > 1 else out[0]), out[-1]


def gram_kernel(a_mine, a_other, b_mine, b_other, *refs):
    panel, gram = refs[-3:-1]
    half, width = a_mine.shape
    quarter = half // 2
    panel[:half, :width] = a_mine[...]
    panel[half:, :width] = a_other[...]
    for k, source in enumerate((b_mine, b_other)):
        panel[k * quarter : (k + 1) * quarter, width:] = source[:quarter, :]
        panel[half + k * quarter : half + (k + 1) * quarter, width:] = source[quarter:, :]
    rows = panel[...]
    gram[...] = dot_tn(rows, rows, HI)


def gram_of(a_mine, a_other, b_mine, b_other, tokens):
    half, width = a_mine.shape
    whole = pl.BlockSpec(memory_space=pltpu.VMEM)
    return pl.pallas_call(
        gram_kernel,
        out_shape=[
            jax.ShapeDtypeStruct((2 * half, 2 * width), F32),
            jax.ShapeDtypeStruct((2 * width, 2 * width), F32),
            MARK,
        ],
        in_specs=[whole] * 4 + [pl.BlockSpec(memory_space=pl.ANY)] * len(tokens),
        out_specs=[whole] * 2 + [pl.BlockSpec(memory_space=pl.ANY)],
        compiler_params=params(24),
        cost_estimate=pl.CostEstimate(
            flops=4 * half * 4 * width * width, bytes_accessed=4 * half * width, transcendentals=0
        ),
    )(a_mine, a_other, b_mine, b_other, *tokens)


def basis_kernel(count, waits, *refs):
    inverse, refs = refs[:count], refs[count:]
    own, other, targets = refs[:3]
    q_high, q_low, basis, turned_high, turned_low = refs[3 + waits :]
    d = pl.program_id(0)
    group, panel = targets.shape[-1], inverse[0].shape[1]
    rows = jnp.concatenate(
        [own[...].reshape(group // 2, panel), other[...].reshape(group // 2, panel)], axis=0
    )
    inv_high, inv_low = halves(inverse[0][...])
    high, low = halves(rows)
    q = dot_nt(inv_high, high) + (dot_nt(inv_low, high) + dot_nt(inv_high, low))
    q_h, q_l = halves(q)
    q_high[...] = q_h
    q_low[...] = q_l
    front = basis.shape[1]
    ids = lax.broadcasted_iota(jnp.int32, (front, group), 0)
    hot = jnp.where(ids == targets[0], 1.0, 0.0).astype(BF16)
    part = dot_nt(q_h, hot) + dot_nt(q_l, hot)

    @pl.when(d == 0)
    def _():
        basis[...] = part

    @pl.when(d > 0)
    def _():
        basis[...] += part

    @pl.when(d == pl.num_programs(0) - 1)
    def _():
        turned_h, turned_l = halves(basis[...].T)
        turned_high[...] = turned_h
        turned_low[...] = turned_l


def basis_rows(inverse, own, other, targets, tokens, front_rows, order):
    last, half, upper, src, panel = own.shape
    n_ct = last * upper
    group = 2 * half * src
    depth = upper.bit_length() - 1

    def place(step):
        d = sum(jnp.where(step == k, value, 0) for k, value in enumerate(order))
        spot = sum(((d >> (k + 1)) & 1) << (depth - 1 - k) for k in range(depth))
        return (d & 1, 0, spot, 0, 0)

    wide = jax.ShapeDtypeStruct((panel, n_ct * group), BF16)
    return pl.pallas_call(
        functools.partial(basis_kernel, len(inverse), len(tokens)),
        grid=(n_ct,),
        out_shape=[
            wide,
            wide,
            jax.ShapeDtypeStruct((panel, front_rows), F32),
            jax.ShapeDtypeStruct((front_rows, panel), BF16),
            jax.ShapeDtypeStruct((front_rows, panel), BF16),
        ],
        in_specs=[
            *[pl.BlockSpec((panel, panel), lambda d: (0, 0)) for _ in inverse],
            pl.BlockSpec((1, half, 1, src, panel), place),
            pl.BlockSpec((1, half, 1, src, panel), place),
            pl.BlockSpec((1, 1, group), lambda d: (d, 0, 0)),
            *[pl.BlockSpec(memory_space=pl.ANY) for _ in tokens],
        ],
        out_specs=[
            pl.BlockSpec((panel, group), lambda d: (0, d)),
            pl.BlockSpec((panel, group), lambda d: (0, d)),
            pl.BlockSpec((panel, front_rows), lambda d: (0, 0)),
            pl.BlockSpec((front_rows, panel), lambda d: (0, 0)),
            pl.BlockSpec((front_rows, panel), lambda d: (0, 0)),
        ],
        compiler_params=params(63),
        cost_estimate=pl.CostEstimate(
            flops=8 * panel * panel * n_ct * group, bytes_accessed=6 * MIB, transcendentals=0
        ),
    )(*inverse, own, other, targets, *tokens)


def mix(q_high, q_low, hot, pieces, spots):
    rows = jnp.concatenate([pieces[n][lo : lo + size, :] for n, lo, size in spots], axis=0)
    high, low = halves(rows)
    factor = dot(q_high[...], high) + (dot(q_low[...], high) + dot(q_high[...], low))
    return factor, dot(hot[...], high) + dot(hot[...], low)


def build_hot(targets, hot):
    @pl.when(pl.program_id(0) == 0)
    def _():
        ids = lax.broadcasted_iota(jnp.int32, hot.shape, 0)
        hot[...] = jnp.where(ids == targets[...], 1.0, 0.0).astype(BF16)


def first_kernel(count, spots, q_high, q_low, targets, *refs):
    pieces, (factor, placed, hot) = refs[:count], refs[-3:]
    build_hot(targets, hot)
    factor[...], placed[...] = mix(q_high, q_low, hot, pieces, spots)


def more_kernel(count, spots, q_high, q_low, targets, factor_in, placed_in, *refs):
    pieces, (factor, placed, hot) = refs[:count], refs[-3:]
    build_hot(targets, hot)
    add_factor, add_placed = mix(q_high, q_low, hot, pieces, spots)
    factor[...] = factor_in[...] + add_factor
    placed[...] = placed_in[...] + add_placed


def last_kernel(count, spots, q_high, q_low, targets, factor_in, placed_in, turned_high, turned_low, *refs):
    pieces, (factor, remainder, hot) = refs[:count], refs[-3:]
    build_hot(targets, hot)
    add_factor, add_placed = mix(q_high, q_low, hot, pieces, spots)
    total = factor_in[...] + add_factor
    factor[...] = total
    high, low = halves(total)
    removed = dot(turned_high[...], high) + (dot(turned_low[...], high) + dot(turned_high[...], low))
    remainder[...] = (placed_in[...] + add_placed) - removed


def mix_call(kernel, group, extra, turned, pieces, spots, q_high, q_low, targets, front_rows, tokens):
    panel = q_high.shape[0]
    block_cols = pieces[0].shape[1]
    depth = sum(size for _, _, size in spots)
    column = lambda j: (0, j)
    fixed = lambda j: (0, group)
    still = lambda j: (0, 0)
    flops = depth * block_cols * (3 * panel + 2 * front_rows)
    flops += 3 * panel * front_rows * block_cols if turned else 0
    return pl.pallas_call(
        functools.partial(kernel, len(pieces), spots),
        grid=(block_cols // WIDE,),
        out_shape=[
            jax.ShapeDtypeStruct((panel, block_cols), F32),
            jax.ShapeDtypeStruct((front_rows, block_cols), F32),
        ],
        in_specs=[
            pl.BlockSpec((panel, depth), fixed),
            pl.BlockSpec((panel, depth), fixed),
            pl.BlockSpec((1, depth), fixed),
        ]
        + [pl.BlockSpec((x.shape[0], WIDE), column) for x in extra]
        + [pl.BlockSpec(x.shape, still) for x in turned]
        + [pl.BlockSpec((x.shape[0], WIDE), column) for x in pieces]
        + [pl.BlockSpec(memory_space=pl.ANY)] * len(tokens),
        out_specs=[
            pl.BlockSpec((panel, WIDE), column),
            pl.BlockSpec((front_rows, WIDE), column),
        ],
        scratch_shapes=[pltpu.VMEM((front_rows, depth), BF16)],
        compiler_params=params(63),
        cost_estimate=pl.CostEstimate(
            flops=flops,
            bytes_accessed=block_cols * (depth + (1 + bool(extra)) * (panel + front_rows)),
            transcendentals=0,
        ),
    )(q_high, q_low, targets, *extra, *turned, *pieces, *tokens)


def shards(children, row_map, column_map, staircase):
    n_rt, n_ct = lax.axis_size("rt"), lax.axis_size("ct")
    my_rt, my_ct = lax.axis_index("rt"), lax.axis_index("ct")
    src, child_cols = children.shape
    total_rows = row_map.shape[0]
    child_rows = total_rows // 2
    front_rows = total_rows // n_rt
    tile_cols = child_cols // staircase.shape[1]
    n_dev = n_rt * n_ct

    first_row = (my_rt * n_ct + my_ct) * src
    which = first_row // child_rows
    first_within = first_row - which * child_rows
    cmap = lax.dynamic_index_in_dim(column_map, which, 0, keepdims=False)
    stairs = lax.dynamic_index_in_dim(staircase, which, 0, keepdims=False)
    limits = jnp.broadcast_to(stairs[:, None], (stairs.shape[0], tile_cols)).reshape(-1)

    edges = STEP * jnp.arange(FRONT_COLS // STEP, dtype=jnp.int32)
    starts = jnp.sum((cmap[None, :] < edges[:, None]).astype(jnp.int32), axis=1)
    starts = jnp.minimum(starts // LANES, (child_cols - STEP - LANES) // LANES)
    info = jnp.concatenate([starts, my_ct[None], first_within[None]]).astype(jnp.int32)
    two, eight = n_ct // 2, n_ct // 8
    near = sorted(range(1, two), key=lambda d: d % 2)
    near = [near[: -2 * eight], near[-2 * eight : -eight], near[-eight:]]
    far = [list(range(two + k * eight, two + (k + 1) * eight)) for k in range(4)]
    order = [0] + near[0] + far[0] + near[1] + far[1] + near[2] + far[2] + far[3]
    spread = functools.partial(widen, info, children, cmap[None, :], limits[None, :], n_ct=n_ct)
    ones = lambda groups: [(d, 1) for group in groups for d in group]
    blocks, mark = spread(ones([near[0]]), tokens=[])

    within = first_within + jnp.arange(src, dtype=jnp.int32)
    panel = jnp.where(within[:, None] < limits[None, :PANEL], children[:, :PANEL], 0.0)
    ct_bits, rt_bits = bits_down(n_ct, 1), bits_down(n_rt, 2)

    rt_order = combos(rt_bits)
    rt_order = rt_order + [r ^ 1 for r in rt_order]
    sources = (my_rt ^ np.array(rt_order, np.int32))[None, :] * n_ct + (
        my_ct ^ np.array(order, np.int32)
    )[:, None]
    targets = row_map.reshape(n_dev, src)[sources.reshape(-1)] - my_rt * front_rows
    targets = targets.reshape(n_ct, 1, n_rt * src)
    flat_targets = targets.reshape(1, total_rows)

    half = n_rt // 2

    def over_ct(group, tokens, part=0):
        operands = gate([blocks[d, part] for d in group], tokens)
        return [swap(x, 0, d) for d, x in zip(group, operands)]

    def over_rt(mine):
        mine = [mine]
        for bit in rt_bits:
            mine = mine + [swap(x, bit, 0) for x in mine]
        return mine

    def one(arrays):
        return arrays[0] if len(arrays) == 1 else join(arrays)[0]

    parts = [panel] + [swap(panel, 0, bits) for bits in combos(ct_bits[:-1])[1:]]
    for bit in rt_bits[:-1]:
        panel, _ = join(parts)
        parts = [panel, swap(panel, bit, 0)]
    (left, right), mark = join(parts, [mark], cut=2)
    near_a = over_ct(near[0], [mark])
    later = ones([[0]] + near[1:] + far[1:]) + [(d, 2) for d in far[0]]
    more, after = spread(later, tokens=[mark])
    blocks |= more
    left, mark = join([left, swap(left, rt_bits[-1], 0)], [after])
    right, _ = join([right, swap(right, 0, ct_bits[-1])])
    far_a = over_ct(far[0], [mark])
    left_other, right_other = swap(left, 0, ct_bits[-1]), swap(right, rt_bits[-1], 0)
    panel, gram, mark = gram_of(left, left_other, right, right_other, near_a + far_a)
    other_gram, other_panel = swap(gram, 1, 0), swap(panel, 1, 0)
    far_e = over_ct(far[0], [mark], 1)
    far_b, near_b = over_ct(far[1], [mark]), over_ct(near[1], [mark])
    joined, after = join([blocks[0, 0]] + near_a + far_a, [mark])
    first = over_rt(joined)
    inverse, mark = inverse_factor(gram, other_gram, [other_panel, after])

    late = list(gate(first + near_b + far_e + far_b, [mark]))
    first, late = late[:half], late[half:]
    far_c, near_c = over_ct(far[2], late[:1]), over_ct(near[2], late[:1])
    joined, mark = join(late[eight : 2 * eight] + late[:eight] + late[2 * eight :])
    second = over_rt(joined)
    inverse = [inverse]
    q_high, q_low, basis, turned_high, turned_low = basis_rows(
        inverse,
        panel.reshape(2, half, n_ct // 2, src, PANEL),
        other_panel.reshape(2, half, n_ct // 2, src, PANEL),
        targets,
        [mark],
        front_rows,
        order,
    )

    call = functools.partial(mix_call, q_high=q_high, q_low=q_low, targets=flat_targets, front_rows=front_rows)
    late = list(gate(first + second + near_c + far_c, [basis]))
    first, second, late = late[:half], late[half : 2 * half], late[2 * half :]
    far_d = over_ct(far[3], late[:1])
    third, fourth = over_rt(one(late[:eight])), over_rt(one(late[eight:]))
    first += [swap(x, 1, 0) for x in first]
    second += [swap(x, 1, 0) for x in second]

    def rows_of(mine, start, size):
        return [(mine + n, start, size) for n in range(n_rt)]

    def group(bundles):
        arrays, spots = [], []
        for mine in bundles:
            for row in range(0, mine[0].shape[0], src):
                spots += rows_of(len(arrays), row, src)
            arrays += mine
        return tuple(arrays), tuple(spots)

    part, height = src // 2, first[0].shape[0]
    whole_rows = height - part * eight
    places = [(n, 0) for n in range(n_rt)]
    spots = [(side, at + row, src) for row in range(0, whole_rows, src) for side, at in places]
    for k in range(eight):
        for n, (side, at) in enumerate(places):
            spots += [(side, at + whole_rows + k * part, part), (n_rt + n, k * part, part)]
    for row in range(part * eight, second[0].shape[0], src):
        spots += rows_of(n_rt, row, src)
    arrays = tuple(first) + tuple(second)
    state = call(first_kernel, 0, (), (), arrays, tuple(spots), tokens=late[:1])
    late = list(gate(third + fourth + far_d, [state[0]]))
    third, fourth, late = late[:half], late[half : 2 * half], late[2 * half :]
    fifth = over_rt(one(late))
    third += [swap(x, 1, 0) for x in third]
    fourth += [swap(x, 1, 0) for x in fourth]
    state = call(more_kernel, 5, tuple(state), (), *group((third,)), tokens=fourth[half:])
    fifth = list(gate(fifth, [state[0]]))
    fifth += [swap(x, 1, 0) for x in fifth]
    turned = (turned_high, turned_low)
    factor, remainder = call(last_kernel, 3, tuple(state), turned, *group((fourth, fifth)), tokens=[])
    return factor, basis, remainder


def solution(mesh):
    placed = (P(("rt", "ct"), None), P(), P(), P())
    return jax.shard_map(
        shards,
        mesh=mesh,
        in_specs=placed,
        out_specs=(P(None, "ct"), P(None, "rt"), P("rt", "ct")),
        check_vma=False,
    )
```

```python
import functools

import jax
import jax.numpy as jnp
import numpy as np
from jax import lax
from jax.experimental import pallas as pl
from jax.experimental.pallas import tpu as pltpu
from jax.sharding import PartitionSpec as P

FRONT_COLS = 16384
PANEL = 512
STEP = 256
WIDE = 512
UNROLL = 8
LANES = 128
NB = 128
SUB = 8

HI = lax.Precision.HIGHEST
F32 = jnp.float32
BF16 = jnp.bfloat16
MIB = 2**20


def swap(x, rt_bit, ct_bit):
    n_rt, n_ct = lax.axis_size("rt"), lax.axis_size("ct")
    if not rt_bit:
        return lax.ppermute(x, "ct", [(c, c ^ ct_bit) for c in range(n_ct)])
    if not ct_bit:
        return lax.ppermute(x, "rt", [(r, r ^ rt_bit) for r in range(n_rt)])
    pairs = [
        (r * n_ct + c, (r ^ rt_bit) * n_ct + (c ^ ct_bit)) for r in range(n_rt) for c in range(n_ct)
    ]
    return lax.ppermute(x, ("rt", "ct"), pairs)


def bits_down(size, last):
    bit, bits = size // 2, []
    while bit >= last:
        bits.append(bit)
        bit //= 2
    return bits


def combos(bits):
    order = [0]
    for bit in bits:
        order = order + [value ^ bit for value in order]
    return order


def halves(x):
    high = x.astype(BF16)
    return high, (x - high.astype(F32)).astype(BF16)


def dot(a, b):
    return jnp.dot(a, b, preferred_element_type=F32)


def dot_nt(a, b, precision=None):
    return lax.dot_general(
        a, b, (((1,), (1,)), ((), ())), precision=precision, preferred_element_type=F32
    )


def dot_tn(a, b, precision=None):
    return lax.dot_general(
        a, b, (((0,), (0,)), ((), ())), precision=precision, preferred_element_type=F32
    )


MARK = jax.ShapeDtypeStruct((SUB, LANES), F32)


def params(mib):
    return pltpu.CompilerParams(vmem_limit_bytes=mib * MIB)


def widen_kernel(tiles, window, places, waits, info, child, cmap, limits, *outs):
    rows = child.shape[0]
    my_block = info[info.shape[0] - 2]
    first_row = info[info.shape[0] - 1]
    row_ids = first_row + lax.broadcasted_iota(jnp.int32, (rows, window), 0)
    col_ids = lax.broadcasted_iota(jnp.int32, (STEP, window), 0)
    made = iter(outs[waits:-1])
    for place, cut in places:
        block = my_block ^ place
        parts = [next(made) for _ in range(cut)]

        def tile(i, carry, block=block, parts=parts):
            t = block * tiles + i
            cols = pl.ds(pl.multiple_of(info[t] * LANES, LANES), window)
            live = jnp.where(row_ids < limits[:, cols], child[:, cols], 0.0)
            hot = jnp.where(col_ids == cmap[:, cols] - t * STEP, 1.0, 0.0).astype(BF16)
            spread = dot_nt(jnp.concatenate(halves(live), axis=0), hot)
            spread = spread[:rows] + spread[rows:]
            there = pl.ds(pl.multiple_of(i * STEP, STEP), STEP)
            height = rows // len(parts)
            for k, part in enumerate(parts):
                part[:, there] = spread[k * height : (k + 1) * height]
            return carry

        lax.fori_loop(0, tiles, tile, 0, unroll=UNROLL)


def widen(info, child, cmap, limits, places, n_ct, tokens):
    rows, width = child.shape
    block_cols = FRONT_COLS // n_ct
    window = STEP + LANES
    whole = pl.BlockSpec(memory_space=pltpu.VMEM)
    made = pl.pallas_call(
        functools.partial(widen_kernel, block_cols // STEP, window, tuple(places), len(tokens)),
        out_shape=[
            jax.ShapeDtypeStruct((rows // cut, block_cols), F32)
            for _, cut in places
            for _ in range(cut)
        ]
        + [MARK],
        in_specs=[pl.BlockSpec(memory_space=pltpu.SMEM), whole, whole, whole]
        + [pl.BlockSpec(memory_space=pl.ANY)] * len(tokens),
        out_specs=[whole] * sum(cut for _, cut in places) + [pl.BlockSpec(memory_space=pl.ANY)],
        compiler_params=params(63),
        cost_estimate=pl.CostEstimate(
            flops=4 * rows * window * block_cols * len(places),
            bytes_accessed=4 * rows * (width + block_cols * len(places)),
            transcendentals=0,
        ),
    )(info, child, cmap, limits, *tokens)
    keys = [(d, k) for d, cut in places for k in range(cut)]
    return dict(zip(keys, made)), made[-1]


def small_inverse(tile):
    a = [
        [jnp.broadcast_to(tile[i : i + 1, k : k + 1], (SUB, NB)) for k in range(i + 1)]
        for i in range(SUB)
    ]
    scale = [None] * SUB
    lower = [[None] * SUB for _ in range(SUB)]
    inverse = [[None] * SUB for _ in range(SUB)]
    for j in range(SUB):
        scale[j] = lax.rsqrt(a[j][j])
        for i in range(j + 1, SUB):
            lower[i][j] = a[i][j] * scale[j]
        for i in range(j + 1, SUB):
            for k in range(j + 1, i + 1):
                a[i][k] = a[i][k] - lower[i][j] * lower[k][j]
    for j in range(SUB):
        inverse[j][j] = scale[j]
        for i in range(j + 1, SUB):
            total = lower[i][j] * inverse[j][j]
            for k in range(j + 1, i):
                total = total + lower[i][k] * inverse[k][j]
            inverse[i][j] = -scale[i] * total
    return inverse


def apply_small(inverse, tiles):
    sub = lax.broadcasted_iota(jnp.int32, (SUB, NB), 0)
    outs = [None] * len(tiles)
    for k in range(SUB):
        column = jnp.zeros((SUB, NB), F32)
        for i in range(k, SUB):
            column = jnp.where(sub == i, inverse[i][k], column)
        for n, tile in enumerate(tiles):
            term = column * jnp.broadcast_to(tile[k : k + 1, :], (SUB, NB))
            outs[n] = term if outs[n] is None else outs[n] + term
    return outs


def identity(n):
    shape = (n, n)
    same = lax.broadcasted_iota(jnp.int32, shape, 0) == lax.broadcasted_iota(jnp.int32, shape, 1)
    return jnp.where(same, 1.0, 0.0)


def thirds(x):
    high = x.astype(BF16)
    rest = x - high.astype(F32)
    mid = rest.astype(BF16)
    return high, mid, (rest - mid.astype(F32)).astype(BF16)


def diagonal_inverse(block, out, work):
    lane = lax.broadcasted_iota(jnp.int32, (SUB, NB), 1)
    work[:NB, :NB] = block
    work[:NB, NB:] = identity(NB)
    work[NB:, :] = jnp.zeros((SUB, 2 * NB), F32)

    def body(s, carry):
        tile, before = carry
        h, m, l = thirds(before)
        left = jnp.concatenate([x[:, :NB] for x in (h, h, m, h, l, m)], axis=0)
        right = jnp.concatenate([h, m, h, l, h, m], axis=0)
        work[:NB, :] = work[:NB, :] - dot_tn(left, right)
        after = work[pl.ds(pl.multiple_of(SUB * s + SUB, SUB), SUB), :]
        shift = lax.rem(NB - SUB * s, NB)
        inverse = small_inverse(pltpu.roll(tile[:, :NB], shift, 1))
        turned = pltpu.roll(after[:, :NB], shift, 1)
        top, top_right = apply_small(inverse, [tile[:, :NB], tile[:, NB:]])
        out[pl.ds(pl.multiple_of(SUB * s, SUB), SUB), :] = top_right
        top = jnp.concatenate([jnp.where(lane >= SUB * s, top, 0.0), top_right], axis=1)
        columns = [jnp.broadcast_to(turned[:, k : k + 1], (SUB, NB)) for k in range(SUB)]
        for i in range(SUB):
            weight = inverse[i][0] * columns[0]
            for k in range(1, i + 1):
                weight = weight + inverse[i][k] * columns[k]
            weight = jnp.concatenate([weight, weight], axis=1)
            after = after - weight * jnp.broadcast_to(top[i : i + 1], (SUB, 2 * NB))
        return after, top

    lax.fori_loop(0, NB // SUB, body, (work[:SUB, :], jnp.zeros((SUB, 2 * NB), F32)))


def factor_kernel(gram_a, gram_b, *refs):
    out, _, whole, small, work = refs[-5:]
    n = out.shape[0]
    whole[:, :n] = gram_a[...] + gram_b[...]
    whole[:, n:] = identity(n)
    for lo in range(0, n, NB):
        hi = lo + NB
        diagonal_inverse(whole[lo:hi, lo:hi], small, work)
        rows = jnp.dot(small[...], whole[lo:hi, lo : n + hi], precision=HI, preferred_element_type=F32)
        out[lo:hi, :hi] = rows[:, n - lo :]
        if hi < n:
            out[lo:hi, hi:] = jnp.zeros((NB, n - hi), F32)
            whole[hi:, hi : n + hi] -= dot_tn(rows[:, NB : n - lo], rows[:, NB:], HI)


def inverse_factor(gram_a, gram_b, tokens):
    n = gram_a.shape[0]
    whole = pl.BlockSpec(memory_space=pltpu.VMEM)
    return pl.pallas_call(
        factor_kernel,
        out_shape=[jax.ShapeDtypeStruct((n, n), F32), MARK],
        in_specs=[whole] * 2 + [pl.BlockSpec(memory_space=pl.ANY)] * len(tokens),
        out_specs=[whole, pl.BlockSpec(memory_space=pl.ANY)],
        scratch_shapes=[
            pltpu.VMEM((n, 2 * n), F32),
            pltpu.VMEM((NB, NB), F32),
            pltpu.VMEM((NB + SUB, 2 * NB), F32),
        ],
        compiler_params=params(63),
        cost_estimate=pl.CostEstimate(
            flops=30 * 10**9, bytes_accessed=12 * n * n, transcendentals=0
        ),
    )(gram_a, gram_b, *tokens)


def gate_kernel(*refs):
    pass


def gate(arrays, tokens):
    if not arrays:
        return []
    anywhere = pl.BlockSpec(memory_space=pl.ANY)
    return pl.pallas_call(
        gate_kernel,
        out_shape=[jax.ShapeDtypeStruct(x.shape, x.dtype) for x in arrays],
        in_specs=[anywhere] * (len(arrays) + len(tokens)),
        out_specs=[anywhere] * len(arrays),
        input_output_aliases={k: k for k in range(len(arrays))},
        cost_estimate=pl.CostEstimate(flops=0, bytes_accessed=0, transcendentals=0),
    )(*arrays, *tokens)


def join_kernel(count, cut, *refs):
    parts, outs = refs[:count], refs[-cut - 1 : -1]
    width = outs[0].shape[1]
    row = 0
    for part in parts:
        rows = part.shape[0]
        for k, out in enumerate(outs):
            out[row : row + rows, :] = part[:, k * width : (k + 1) * width]
        row += rows


def join(parts, tokens=(), cut=1):
    rows, width = sum(x.shape[0] for x in parts), parts[0].shape[1]
    whole = pl.BlockSpec(memory_space=pltpu.VMEM)
    out = pl.pallas_call(
        functools.partial(join_kernel, len(parts), cut),
        out_shape=[jax.ShapeDtypeStruct((rows, width // cut), F32)] * cut + [MARK],
        in_specs=[whole] * len(parts) + [pl.BlockSpec(memory_space=pl.ANY)] * len(tokens),
        out_specs=[whole] * cut + [pl.BlockSpec(memory_space=pl.ANY)],
        compiler_params=params(16 if width <= PANEL else 63),
        cost_estimate=pl.CostEstimate(
            flops=0, bytes_accessed=8 * rows * width, transcendentals=0
        ),
    )(*parts, *tokens)
    return (out[:cut] if cut > 1 else out[0]), out[-1]


def gram_kernel(a_mine, a_other, b_mine, b_other, *refs):
    panel, gram = refs[-3:-1]
    half, width = a_mine.shape
    quarter = half // 2
    panel[:half, :width] = a_mine[...]
    panel[half:, :width] = a_other[...]
    for k, source in enumerate((b_mine, b_other)):
        panel[k * quarter : (k + 1) * quarter, width:] = source[:quarter, :]
        panel[half + k * quarter : half + (k + 1) * quarter, width:] = source[quarter:, :]
    rows = panel[...]
    gram[...] = dot_tn(rows, rows, HI)


def gram_of(a_mine, a_other, b_mine, b_other, tokens):
    half, width = a_mine.shape
    whole = pl.BlockSpec(memory_space=pltpu.VMEM)
    return pl.pallas_call(
        gram_kernel,
        out_shape=[
            jax.ShapeDtypeStruct((2 * half, 2 * width), F32),
            jax.ShapeDtypeStruct((2 * width, 2 * width), F32),
            MARK,
        ],
        in_specs=[whole] * 4 + [pl.BlockSpec(memory_space=pl.ANY)] * len(tokens),
        out_specs=[whole] * 2 + [pl.BlockSpec(memory_space=pl.ANY)],
        compiler_params=params(24),
        cost_estimate=pl.CostEstimate(
            flops=4 * half * 4 * width * width, bytes_accessed=4 * half * width, transcendentals=0
        ),
    )(a_mine, a_other, b_mine, b_other, *tokens)


def basis_kernel(count, waits, *refs):
    inverse, refs = refs[:count], refs[count:]
    own, other, targets = refs[:3]
    q_high, q_low, basis, turned_high, turned_low = refs[3 + waits :]
    d = pl.program_id(0)
    group, panel = targets.shape[-1], inverse[0].shape[1]
    rows = jnp.concatenate(
        [own[...].reshape(group // 2, panel), other[...].reshape(group // 2, panel)], axis=0
    )
    inv_high, inv_low = halves(inverse[0][...])
    high, low = halves(rows)
    q = dot_nt(inv_high, high) + (dot_nt(inv_low, high) + dot_nt(inv_high, low))
    q_h, q_l = halves(q)
    q_high[...] = q_h
    q_low[...] = q_l
    front = basis.shape[1]
    ids = lax.broadcasted_iota(jnp.int32, (front, group), 0)
    hot = jnp.where(ids == targets[0], 1.0, 0.0).astype(BF16)
    part = dot_nt(q_h, hot) + dot_nt(q_l, hot)

    @pl.when(d == 0)
    def _():
        basis[...] = part

    @pl.when(d > 0)
    def _():
        basis[...] += part

    @pl.when(d == pl.num_programs(0) - 1)
    def _():
        turned_h, turned_l = halves(basis[...].T)
        turned_high[...] = turned_h
        turned_low[...] = turned_l


def basis_rows(inverse, own, other, targets, tokens, front_rows, order):
    last, half, upper, src, panel = own.shape
    n_ct = last * upper
    group = 2 * half * src
    depth = upper.bit_length() - 1

    def place(step):
        d = sum(jnp.where(step == k, value, 0) for k, value in enumerate(order))
        spot = sum(((d >> (k + 1)) & 1) << (depth - 1 - k) for k in range(depth))
        return (d & 1, 0, spot, 0, 0)

    wide = jax.ShapeDtypeStruct((panel, n_ct * group), BF16)
    return pl.pallas_call(
        functools.partial(basis_kernel, len(inverse), len(tokens)),
        grid=(n_ct,),
        out_shape=[
            wide,
            wide,
            jax.ShapeDtypeStruct((panel, front_rows), F32),
            jax.ShapeDtypeStruct((front_rows, panel), BF16),
            jax.ShapeDtypeStruct((front_rows, panel), BF16),
        ],
        in_specs=[
            *[pl.BlockSpec((panel, panel), lambda d: (0, 0)) for _ in inverse],
            pl.BlockSpec((1, half, 1, src, panel), place),
            pl.BlockSpec((1, half, 1, src, panel), place),
            pl.BlockSpec((1, 1, group), lambda d: (d, 0, 0)),
            *[pl.BlockSpec(memory_space=pl.ANY) for _ in tokens],
        ],
        out_specs=[
            pl.BlockSpec((panel, group), lambda d: (0, d)),
            pl.BlockSpec((panel, group), lambda d: (0, d)),
            pl.BlockSpec((panel, front_rows), lambda d: (0, 0)),
            pl.BlockSpec((front_rows, panel), lambda d: (0, 0)),
            pl.BlockSpec((front_rows, panel), lambda d: (0, 0)),
        ],
        compiler_params=params(63),
        cost_estimate=pl.CostEstimate(
            flops=8 * panel * panel * n_ct * group, bytes_accessed=6 * MIB, transcendentals=0
        ),
    )(*inverse, own, other, targets, *tokens)


def mix(q_high, q_low, hot, pieces, spots):
    rows = jnp.concatenate([pieces[n][lo : lo + size, :] for n, lo, size in spots], axis=0)
    high, low = halves(rows)
    factor = dot(q_high[...], high) + (dot(q_low[...], high) + dot(q_high[...], low))
    return factor, dot(hot[...], high) + dot(hot[...], low)


def build_hot(targets, hot):
    @pl.when(pl.program_id(0) == 0)
    def _():
        ids = lax.broadcasted_iota(jnp.int32, hot.shape, 0)
        hot[...] = jnp.where(ids == targets[...], 1.0, 0.0).astype(BF16)


def first_kernel(count, spots, q_high, q_low, targets, *refs):
    pieces, (factor, placed, hot) = refs[:count], refs[-3:]
    build_hot(targets, hot)
    factor[...], placed[...] = mix(q_high, q_low, hot, pieces, spots)


def more_kernel(count, spots, q_high, q_low, targets, factor_in, placed_in, *refs):
    pieces, (factor, placed, hot) = refs[:count], refs[-3:]
    build_hot(targets, hot)
    add_factor, add_placed = mix(q_high, q_low, hot, pieces, spots)
    factor[...] = factor_in[...] + add_factor
    placed[...] = placed_in[...] + add_placed


def last_kernel(count, spots, q_high, q_low, targets, factor_in, placed_in, turned_high, turned_low, *refs):
    pieces, (factor, remainder, hot) = refs[:count], refs[-3:]
    build_hot(targets, hot)
    add_factor, add_placed = mix(q_high, q_low, hot, pieces, spots)
    total = factor_in[...] + add_factor
    factor[...] = total
    high, low = halves(total)
    removed = dot(turned_high[...], high) + (dot(turned_low[...], high) + dot(turned_high[...], low))
    remainder[...] = (placed_in[...] + add_placed) - removed


def mix_call(kernel, group, extra, turned, pieces, spots, q_high, q_low, targets, front_rows, tokens):
    panel = q_high.shape[0]
    block_cols = pieces[0].shape[1]
    depth = sum(size for _, _, size in spots)
    column = lambda j: (0, j)
    fixed = lambda j: (0, group)
    still = lambda j: (0, 0)
    flops = depth * block_cols * (3 * panel + 2 * front_rows)
    flops += 3 * panel * front_rows * block_cols if turned else 0
    return pl.pallas_call(
        functools.partial(kernel, len(pieces), spots),
        grid=(block_cols // WIDE,),
        out_shape=[
            jax.ShapeDtypeStruct((panel, block_cols), F32),
            jax.ShapeDtypeStruct((front_rows, block_cols), F32),
        ],
        in_specs=[
            pl.BlockSpec((panel, depth), fixed),
            pl.BlockSpec((panel, depth), fixed),
            pl.BlockSpec((1, depth), fixed),
        ]
        + [pl.BlockSpec((x.shape[0], WIDE), column) for x in extra]
        + [pl.BlockSpec(x.shape, still) for x in turned]
        + [pl.BlockSpec((x.shape[0], WIDE), column) for x in pieces]
        + [pl.BlockSpec(memory_space=pl.ANY)] * len(tokens),
        out_specs=[
            pl.BlockSpec((panel, WIDE), column),
            pl.BlockSpec((front_rows, WIDE), column),
        ],
        scratch_shapes=[pltpu.VMEM((front_rows, depth), BF16)],
        compiler_params=params(63),
        cost_estimate=pl.CostEstimate(
            flops=flops,
            bytes_accessed=block_cols * (depth + (1 + bool(extra)) * (panel + front_rows)),
            transcendentals=0,
        ),
    )(q_high, q_low, targets, *extra, *turned, *pieces, *tokens)


def shards(children, row_map, column_map, staircase):
    n_rt, n_ct = lax.axis_size("rt"), lax.axis_size("ct")
    my_rt, my_ct = lax.axis_index("rt"), lax.axis_index("ct")
    src, child_cols = children.shape
    total_rows = row_map.shape[0]
    child_rows = total_rows // 2
    front_rows = total_rows // n_rt
    tile_cols = child_cols // staircase.shape[1]
    n_dev = n_rt * n_ct

    first_row = (my_rt * n_ct + my_ct) * src
    which = first_row // child_rows
    first_within = first_row - which * child_rows
    cmap = lax.dynamic_index_in_dim(column_map, which, 0, keepdims=False)
    stairs = lax.dynamic_index_in_dim(staircase, which, 0, keepdims=False)
    limits = jnp.broadcast_to(stairs[:, None], (stairs.shape[0], tile_cols)).reshape(-1)

    edges = STEP * jnp.arange(FRONT_COLS // STEP, dtype=jnp.int32)
    starts = jnp.sum((cmap[None, :] < edges[:, None]).astype(jnp.int32), axis=1)
    starts = jnp.minimum(starts // LANES, (child_cols - STEP - LANES) // LANES)
    info = jnp.concatenate([starts, my_ct[None], first_within[None]]).astype(jnp.int32)
    two, eight = n_ct // 2, n_ct // 8
    near = sorted(range(1, two), key=lambda d: d % 2)
    near = [near[: -2 * eight], near[-2 * eight : -eight], near[-eight:]]
    far = [list(range(two + k * eight, two + (k + 1) * eight)) for k in range(4)]
    order = [0] + near[0] + far[0] + near[1] + far[1] + near[2] + far[2] + far[3]
    spread = functools.partial(widen, info, children, cmap[None, :], limits[None, :], n_ct=n_ct)
    ones = lambda groups: [(d, 1) for group in groups for d in group]
    blocks, mark = spread(ones([near[0]]), tokens=[])

    within = first_within + jnp.arange(src, dtype=jnp.int32)
    panel = jnp.where(within[:, None] < limits[None, :PANEL], children[:, :PANEL], 0.0)
    ct_bits, rt_bits = bits_down(n_ct, 1), bits_down(n_rt, 2)

    rt_order = combos(rt_bits)
    rt_order = rt_order + [r ^ 1 for r in rt_order]
    sources = (my_rt ^ np.array(rt_order, np.int32))[None, :] * n_ct + (
        my_ct ^ np.array(order, np.int32)
    )[:, None]
    targets = row_map.reshape(n_dev, src)[sources.reshape(-1)] - my_rt * front_rows
    targets = targets.reshape(n_ct, 1, n_rt * src)
    flat_targets = targets.reshape(1, total_rows)

    half = n_rt // 2

    def over_ct(group, tokens, part=0):
        operands = gate([blocks[d, part] for d in group], tokens)
        return [swap(x, 0, d) for d, x in zip(group, operands)]

    def over_rt(mine):
        mine = [mine]
        for bit in rt_bits:
            mine = mine + [swap(x, bit, 0) for x in mine]
        return mine

    def one(arrays):
        return arrays[0] if len(arrays) == 1 else join(arrays)[0]

    parts = [panel] + [swap(panel, 0, bits) for bits in combos(ct_bits[:-1])[1:]]
    for bit in rt_bits[:-1]:
        panel, _ = join(parts)
        parts = [panel, swap(panel, bit, 0)]
    (left, right), mark = join(parts, [mark], cut=2)
    near_a = over_ct(near[0], [mark])
    later = ones([[0]] + near[1:] + far[1:]) + [(d, 2) for d in far[0]]
    more, after = spread(later, tokens=[mark])
    blocks |= more
    left, mark = join([left, swap(left, rt_bits[-1], 0)], [after])
    right, _ = join([right, swap(right, 0, ct_bits[-1])])
    far_a = over_ct(far[0], [mark])
    left_other, right_other = swap(left, 0, ct_bits[-1]), swap(right, rt_bits[-1], 0)
    panel, gram, mark = gram_of(left, left_other, right, right_other, near_a + far_a)
    other_gram, other_panel = swap(gram, 1, 0), swap(panel, 1, 0)
    far_e = over_ct(far[0], [mark], 1)
    far_b, near_b = over_ct(far[1], [mark]), over_ct(near[1], [mark])
    joined, after = join([blocks[0, 0]] + near_a + far_a, [mark])
    first = over_rt(joined)
    inverse, mark = inverse_factor(gram, other_gram, [other_panel, after])

    late = list(gate(first + near_b + far_e + far_b, [mark]))
    first, late = late[:half], late[half:]
    far_c, near_c = over_ct(far[2], late[:1]), over_ct(near[2], late[:1])
    joined, mark = join(late[eight : 2 * eight] + late[:eight] + late[2 * eight :])
    second = over_rt(joined)
    crossed = swap(first[0], 1, 0)
    inverse = [inverse]
    q_high, q_low, basis, turned_high, turned_low = basis_rows(
        inverse,
        panel.reshape(2, half, n_ct // 2, src, PANEL),
        other_panel.reshape(2, half, n_ct // 2, src, PANEL),
        targets,
        [mark],
        front_rows,
        order,
    )

    call = functools.partial(mix_call, q_high=q_high, q_low=q_low, targets=flat_targets, front_rows=front_rows)
    late = list(gate(first + [crossed] + second + near_c + far_c, [basis]))
    crossed = late.pop(half)
    first, second, late = late[:half], late[half : 2 * half], late[2 * half :]
    far_d = over_ct(far[3], late[:1])
    third, fourth = over_rt(one(late[:eight])), over_rt(one(late[eight:]))
    first += [crossed] + [swap(x, 1, 0) for x in first[1:]]
    second += [swap(x, 1, 0) for x in second]

    def rows_of(mine, start, size):
        return [(mine + n, start, size) for n in range(n_rt)]

    def group(bundles):
        arrays, spots = [], []
        for mine in bundles:
            for row in range(0, mine[0].shape[0], src):
                spots += rows_of(len(arrays), row, src)
            arrays += mine
        return tuple(arrays), tuple(spots)

    part, height = src // 2, first[0].shape[0]
    whole_rows = height - part * eight
    places = [(n, 0) for n in range(n_rt)]
    spots = [(side, at + row, src) for row in range(0, whole_rows, src) for side, at in places]
    for k in range(eight):
        for n, (side, at) in enumerate(places):
            spots += [(side, at + whole_rows + k * part, part), (n_rt + n, k * part, part)]
    for row in range(part * eight, second[0].shape[0], src):
        spots += rows_of(n_rt, row, src)
    arrays = tuple(first) + tuple(second)
    state = call(first_kernel, 0, (), (), arrays, tuple(spots), tokens=late[:1])
    late = list(gate(third + fourth + far_d, [state[0]]))
    third, fourth, late = late[:half], late[half : 2 * half], late[2 * half :]
    fifth = over_rt(one(late))
    third += [swap(x, 1, 0) for x in third]
    fourth += [swap(x, 1, 0) for x in fourth]
    state = call(more_kernel, 5, tuple(state), (), *group((third,)), tokens=fourth[half:])
    fifth = list(gate(fifth, [state[0]]))
    fifth += [swap(x, 1, 0) for x in fifth]
    turned = (turned_high, turned_low)
    factor, remainder = call(last_kernel, 3, tuple(state), turned, *group((fourth, fifth)), tokens=[])
    return factor, basis, remainder


def solution(mesh):
    placed = (P(("rt", "ct"), None), P(), P(), P())
    return jax.shard_map(
        shards,
        mesh=mesh,
        in_specs=placed,
        out_specs=(P(None, "ct"), P(None, "rt"), P("rt", "ct")),
        check_vma=False,
    )
```

```python
import functools

import jax
import jax.numpy as jnp
import numpy as np
from jax import lax
from jax.experimental import pallas as pl
from jax.experimental.pallas import tpu as pltpu
from jax.sharding import PartitionSpec as P

FRONT_COLS = 16384
PANEL = 512
STEP = 256
WIDE = 512
UNROLL = 8
LANES = 128
NB = 128
SUB = 8

HI = lax.Precision.HIGHEST
F32 = jnp.float32
BF16 = jnp.bfloat16
MIB = 2**20


def swap(x, rt_bit, ct_bit):
    n_rt, n_ct = lax.axis_size("rt"), lax.axis_size("ct")
    if not rt_bit:
        return lax.ppermute(x, "ct", [(c, c ^ ct_bit) for c in range(n_ct)])
    if not ct_bit:
        return lax.ppermute(x, "rt", [(r, r ^ rt_bit) for r in range(n_rt)])
    pairs = [
        (r * n_ct + c, (r ^ rt_bit) * n_ct + (c ^ ct_bit)) for r in range(n_rt) for c in range(n_ct)
    ]
    return lax.ppermute(x, ("rt", "ct"), pairs)


def bits_down(size, last):
    bit, bits = size // 2, []
    while bit >= last:
        bits.append(bit)
        bit //= 2
    return bits


def combos(bits):
    order = [0]
    for bit in bits:
        order = order + [value ^ bit for value in order]
    return order


def halves(x):
    high = x.astype(BF16)
    return high, (x - high.astype(F32)).astype(BF16)


def dot(a, b):
    return jnp.dot(a, b, preferred_element_type=F32)


def dot_nt(a, b, precision=None):
    return lax.dot_general(
        a, b, (((1,), (1,)), ((), ())), precision=precision, preferred_element_type=F32
    )


def dot_tn(a, b, precision=None):
    return lax.dot_general(
        a, b, (((0,), (0,)), ((), ())), precision=precision, preferred_element_type=F32
    )


MARK = jax.ShapeDtypeStruct((SUB, LANES), F32)


def params(mib):
    return pltpu.CompilerParams(vmem_limit_bytes=mib * MIB)


def widen_kernel(tiles, window, places, waits, info, child, cmap, limits, *outs):
    rows = child.shape[0]
    my_block = info[info.shape[0] - 2]
    first_row = info[info.shape[0] - 1]
    row_ids = first_row + lax.broadcasted_iota(jnp.int32, (rows, window), 0)
    col_ids = lax.broadcasted_iota(jnp.int32, (STEP, window), 0)
    made = iter(outs[waits:-1])
    for place, cut in places:
        block = my_block ^ place
        parts = [next(made) for _ in range(cut)]

        def tile(i, carry, block=block, parts=parts):
            t = block * tiles + i
            cols = pl.ds(pl.multiple_of(info[t] * LANES, LANES), window)
            live = jnp.where(row_ids < limits[:, cols], child[:, cols], 0.0)
            hot = jnp.where(col_ids == cmap[:, cols] - t * STEP, 1.0, 0.0).astype(BF16)
            spread = dot_nt(jnp.concatenate(halves(live), axis=0), hot)
            spread = spread[:rows] + spread[rows:]
            there = pl.ds(pl.multiple_of(i * STEP, STEP), STEP)
            height = rows // len(parts)
            for k, part in enumerate(parts):
                part[:, there] = spread[k * height : (k + 1) * height]
            return carry

        lax.fori_loop(0, tiles, tile, 0, unroll=UNROLL)


def widen(info, child, cmap, limits, places, n_ct, tokens):
    rows, width = child.shape
    block_cols = FRONT_COLS // n_ct
    window = STEP + LANES
    whole = pl.BlockSpec(memory_space=pltpu.VMEM)
    made = pl.pallas_call(
        functools.partial(widen_kernel, block_cols // STEP, window, tuple(places), len(tokens)),
        out_shape=[
            jax.ShapeDtypeStruct((rows // cut, block_cols), F32)
            for _, cut in places
            for _ in range(cut)
        ]
        + [MARK],
        in_specs=[pl.BlockSpec(memory_space=pltpu.SMEM), whole, whole, whole]
        + [pl.BlockSpec(memory_space=pl.ANY)] * len(tokens),
        out_specs=[whole] * sum(cut for _, cut in places) + [pl.BlockSpec(memory_space=pl.ANY)],
        compiler_params=params(63),
        cost_estimate=pl.CostEstimate(
            flops=4 * rows * window * block_cols * len(places),
            bytes_accessed=4 * rows * (width + block_cols * len(places)),
            transcendentals=0,
        ),
    )(info, child, cmap, limits, *tokens)
    keys = [(d, k) for d, cut in places for k in range(cut)]
    return dict(zip(keys, made)), made[-1]


def small_inverse(tile):
    a = [
        [jnp.broadcast_to(tile[i : i + 1, k : k + 1], (SUB, NB)) for k in range(i + 1)]
        for i in range(SUB)
    ]
    scale = [None] * SUB
    lower = [[None] * SUB for _ in range(SUB)]
    inverse = [[None] * SUB for _ in range(SUB)]
    for j in range(SUB):
        scale[j] = lax.rsqrt(a[j][j])
        for i in range(j + 1, SUB):
            lower[i][j] = a[i][j] * scale[j]
        for i in range(j + 1, SUB):
            for k in range(j + 1, i + 1):
                a[i][k] = a[i][k] - lower[i][j] * lower[k][j]
    for j in range(SUB):
        inverse[j][j] = scale[j]
        for i in range(j + 1, SUB):
            total = lower[i][j] * inverse[j][j]
            for k in range(j + 1, i):
                total = total + lower[i][k] * inverse[k][j]
            inverse[i][j] = -scale[i] * total
    return inverse


def apply_small(inverse, tiles):
    sub = lax.broadcasted_iota(jnp.int32, (SUB, NB), 0)
    outs = [None] * len(tiles)
    for k in range(SUB):
        column = jnp.zeros((SUB, NB), F32)
        for i in range(k, SUB):
            column = jnp.where(sub == i, inverse[i][k], column)
        for n, tile in enumerate(tiles):
            term = column * jnp.broadcast_to(tile[k : k + 1, :], (SUB, NB))
            outs[n] = term if outs[n] is None else outs[n] + term
    return outs


def identity(n):
    shape = (n, n)
    same = lax.broadcasted_iota(jnp.int32, shape, 0) == lax.broadcasted_iota(jnp.int32, shape, 1)
    return jnp.where(same, 1.0, 0.0)


def thirds(x):
    high = x.astype(BF16)
    rest = x - high.astype(F32)
    mid = rest.astype(BF16)
    return high, mid, (rest - mid.astype(F32)).astype(BF16)


def diagonal_inverse(block, out, work):
    lane = lax.broadcasted_iota(jnp.int32, (SUB, NB), 1)
    work[:NB, :NB] = block
    work[:NB, NB:] = identity(NB)
    work[NB:, :] = jnp.zeros((SUB, 2 * NB), F32)

    def body(s, carry):
        tile, before = carry
        h, m, l = thirds(before)
        left = jnp.concatenate([x[:, :NB] for x in (h, h, m, h, l, m)], axis=0)
        right = jnp.concatenate([h, m, h, l, h, m], axis=0)
        work[:NB, :] = work[:NB, :] - dot_tn(left, right)
        after = work[pl.ds(pl.multiple_of(SUB * s + SUB, SUB), SUB), :]
        shift = lax.rem(NB - SUB * s, NB)
        inverse = small_inverse(pltpu.roll(tile[:, :NB], shift, 1))
        turned = pltpu.roll(after[:, :NB], shift, 1)
        top, top_right = apply_small(inverse, [tile[:, :NB], tile[:, NB:]])
        out[pl.ds(pl.multiple_of(SUB * s, SUB), SUB), :] = top_right
        top = jnp.concatenate([jnp.where(lane >= SUB * s, top, 0.0), top_right], axis=1)
        columns = [jnp.broadcast_to(turned[:, k : k + 1], (SUB, NB)) for k in range(SUB)]
        for i in range(SUB):
            weight = inverse[i][0] * columns[0]
            for k in range(1, i + 1):
                weight = weight + inverse[i][k] * columns[k]
            weight = jnp.concatenate([weight, weight], axis=1)
            after = after - weight * jnp.broadcast_to(top[i : i + 1], (SUB, 2 * NB))
        return after, top

    start = (work[:SUB, :], jnp.zeros((SUB, 2 * NB), F32))
    lax.fori_loop(0, NB // SUB, body, start, unroll=2)


def factor_kernel(gram_a, gram_b, *refs):
    out, _, whole, small, work = refs[-5:]
    n = out.shape[0]
    whole[:, :n] = gram_a[...] + gram_b[...]
    whole[:, n:] = identity(n)
    for lo in range(0, n, NB):
        hi = lo + NB
        diagonal_inverse(whole[lo:hi, lo:hi], small, work)
        rows = jnp.dot(small[...], whole[lo:hi, lo : n + hi], precision=HI, preferred_element_type=F32)
        out[lo:hi, :hi] = rows[:, n - lo :]
        if hi < n:
            out[lo:hi, hi:] = jnp.zeros((NB, n - hi), F32)
            whole[hi:, hi : n + hi] -= dot_tn(rows[:, NB : n - lo], rows[:, NB:], HI)


def inverse_factor(gram_a, gram_b, tokens):
    n = gram_a.shape[0]
    whole = pl.BlockSpec(memory_space=pltpu.VMEM)
    return pl.pallas_call(
        factor_kernel,
        out_shape=[jax.ShapeDtypeStruct((n, n), F32), MARK],
        in_specs=[whole] * 2 + [pl.BlockSpec(memory_space=pl.ANY)] * len(tokens),
        out_specs=[whole, pl.BlockSpec(memory_space=pl.ANY)],
        scratch_shapes=[
            pltpu.VMEM((n, 2 * n), F32),
            pltpu.VMEM((NB, NB), F32),
            pltpu.VMEM((NB + SUB, 2 * NB), F32),
        ],
        compiler_params=params(63),
        cost_estimate=pl.CostEstimate(
            flops=30 * 10**9, bytes_accessed=12 * n * n, transcendentals=0
        ),
    )(gram_a, gram_b, *tokens)


def gate_kernel(*refs):
    pass


def gate(arrays, tokens):
    if not arrays:
        return []
    anywhere = pl.BlockSpec(memory_space=pl.ANY)
    return pl.pallas_call(
        gate_kernel,
        out_shape=[jax.ShapeDtypeStruct(x.shape, x.dtype) for x in arrays],
        in_specs=[anywhere] * (len(arrays) + len(tokens)),
        out_specs=[anywhere] * len(arrays),
        input_output_aliases={k: k for k in range(len(arrays))},
        cost_estimate=pl.CostEstimate(flops=0, bytes_accessed=0, transcendentals=0),
    )(*arrays, *tokens)


def join_kernel(count, cut, *refs):
    parts, outs = refs[:count], refs[-cut - 1 : -1]
    width = outs[0].shape[1]
    row = 0
    for part in parts:
        rows = part.shape[0]
        for k, out in enumerate(outs):
            out[row : row + rows, :] = part[:, k * width : (k + 1) * width]
        row += rows


def join(parts, tokens=(), cut=1):
    rows, width = sum(x.shape[0] for x in parts), parts[0].shape[1]
    whole = pl.BlockSpec(memory_space=pltpu.VMEM)
    out = pl.pallas_call(
        functools.partial(join_kernel, len(parts), cut),
        out_shape=[jax.ShapeDtypeStruct((rows, width // cut), F32)] * cut + [MARK],
        in_specs=[whole] * len(parts) + [pl.BlockSpec(memory_space=pl.ANY)] * len(tokens),
        out_specs=[whole] * cut + [pl.BlockSpec(memory_space=pl.ANY)],
        compiler_params=params(16 if width <= PANEL else 63),
        cost_estimate=pl.CostEstimate(
            flops=0, bytes_accessed=8 * rows * width, transcendentals=0
        ),
    )(*parts, *tokens)
    return (out[:cut] if cut > 1 else out[0]), out[-1]


def gram_kernel(a_mine, a_other, b_mine, b_other, *refs):
    panel, gram = refs[-3:-1]
    half, width = a_mine.shape
    quarter = half // 2
    panel[:half, :width] = a_mine[...]
    panel[half:, :width] = a_other[...]
    for k, source in enumerate((b_mine, b_other)):
        panel[k * quarter : (k + 1) * quarter, width:] = source[:quarter, :]
        panel[half + k * quarter : half + (k + 1) * quarter, width:] = source[quarter:, :]
    rows = panel[...]
    gram[...] = dot_tn(rows, rows, HI)


def gram_of(a_mine, a_other, b_mine, b_other, tokens):
    half, width = a_mine.shape
    whole = pl.BlockSpec(memory_space=pltpu.VMEM)
    return pl.pallas_call(
        gram_kernel,
        out_shape=[
            jax.ShapeDtypeStruct((2 * half, 2 * width), F32),
            jax.ShapeDtypeStruct((2 * width, 2 * width), F32),
            MARK,
        ],
        in_specs=[whole] * 4 + [pl.BlockSpec(memory_space=pl.ANY)] * len(tokens),
        out_specs=[whole] * 2 + [pl.BlockSpec(memory_space=pl.ANY)],
        compiler_params=params(24),
        cost_estimate=pl.CostEstimate(
            flops=4 * half * 4 * width * width, bytes_accessed=4 * half * width, transcendentals=0
        ),
    )(a_mine, a_other, b_mine, b_other, *tokens)


def basis_kernel(count, waits, *refs):
    inverse, refs = refs[:count], refs[count:]
    own, other, targets = refs[:3]
    q_high, q_low, basis, turned_high, turned_low = refs[3 + waits :]
    d = pl.program_id(0)
    group, panel = targets.shape[-1], inverse[0].shape[1]
    rows = jnp.concatenate(
        [own[...].reshape(group // 2, panel), other[...].reshape(group // 2, panel)], axis=0
    )
    inv_high, inv_low = halves(inverse[0][...])
    high, low = halves(rows)
    q = dot_nt(inv_high, high) + (dot_nt(inv_low, high) + dot_nt(inv_high, low))
    q_h, q_l = halves(q)
    q_high[...] = q_h
    q_low[...] = q_l
    front = basis.shape[1]
    ids = lax.broadcasted_iota(jnp.int32, (front, group), 0)
    hot = jnp.where(ids == targets[0], 1.0, 0.0).astype(BF16)
    part = dot_nt(q_h, hot) + dot_nt(q_l, hot)

    @pl.when(d == 0)
    def _():
        basis[...] = part

    @pl.when(d > 0)
    def _():
        basis[...] += part

    @pl.when(d == pl.num_programs(0) - 1)
    def _():
        turned_h, turned_l = halves(basis[...].T)
        turned_high[...] = turned_h
        turned_low[...] = turned_l


def basis_rows(inverse, own, other, targets, tokens, front_rows, order):
    last, half, upper, src, panel = own.shape
    n_ct = last * upper
    group = 2 * half * src
    depth = upper.bit_length() - 1

    def place(step):
        d = sum(jnp.where(step == k, value, 0) for k, value in enumerate(order))
        spot = sum(((d >> (k + 1)) & 1) << (depth - 1 - k) for k in range(depth))
        return (d & 1, 0, spot, 0, 0)

    wide = jax.ShapeDtypeStruct((panel, n_ct * group), BF16)
    return pl.pallas_call(
        functools.partial(basis_kernel, len(inverse), len(tokens)),
        grid=(n_ct,),
        out_shape=[
            wide,
            wide,
            jax.ShapeDtypeStruct((panel, front_rows), F32),
            jax.ShapeDtypeStruct((front_rows, panel), BF16),
            jax.ShapeDtypeStruct((front_rows, panel), BF16),
        ],
        in_specs=[
            *[pl.BlockSpec((panel, panel), lambda d: (0, 0)) for _ in inverse],
            pl.BlockSpec((1, half, 1, src, panel), place),
            pl.BlockSpec((1, half, 1, src, panel), place),
            pl.BlockSpec((1, 1, group), lambda d: (d, 0, 0)),
            *[pl.BlockSpec(memory_space=pl.ANY) for _ in tokens],
        ],
        out_specs=[
            pl.BlockSpec((panel, group), lambda d: (0, d)),
            pl.BlockSpec((panel, group), lambda d: (0, d)),
            pl.BlockSpec((panel, front_rows), lambda d: (0, 0)),
            pl.BlockSpec((front_rows, panel), lambda d: (0, 0)),
            pl.BlockSpec((front_rows, panel), lambda d: (0, 0)),
        ],
        compiler_params=params(63),
        cost_estimate=pl.CostEstimate(
            flops=8 * panel * panel * n_ct * group, bytes_accessed=6 * MIB, transcendentals=0
        ),
    )(*inverse, own, other, targets, *tokens)


def mix(q_high, q_low, hot, pieces, spots):
    rows = jnp.concatenate([pieces[n][lo : lo + size, :] for n, lo, size in spots], axis=0)
    high, low = halves(rows)
    factor = dot(q_high[...], high) + (dot(q_low[...], high) + dot(q_high[...], low))
    return factor, dot(hot[...], high) + dot(hot[...], low)


def build_hot(targets, hot):
    @pl.when(pl.program_id(0) == 0)
    def _():
        ids = lax.broadcasted_iota(jnp.int32, hot.shape, 0)
        hot[...] = jnp.where(ids == targets[...], 1.0, 0.0).astype(BF16)


def first_kernel(count, spots, q_high, q_low, targets, *refs):
    pieces, (factor, placed, hot) = refs[:count], refs[-3:]
    build_hot(targets, hot)
    factor[...], placed[...] = mix(q_high, q_low, hot, pieces, spots)


def more_kernel(count, spots, q_high, q_low, targets, factor_in, placed_in, *refs):
    pieces, (factor, placed, hot) = refs[:count], refs[-3:]
    build_hot(targets, hot)
    add_factor, add_placed = mix(q_high, q_low, hot, pieces, spots)
    factor[...] = factor_in[...] + add_factor
    placed[...] = placed_in[...] + add_placed


def last_kernel(count, spots, q_high, q_low, targets, factor_in, placed_in, turned_high, turned_low, *refs):
    pieces, (factor, remainder, hot) = refs[:count], refs[-3:]
    build_hot(targets, hot)
    add_factor, add_placed = mix(q_high, q_low, hot, pieces, spots)
    total = factor_in[...] + add_factor
    factor[...] = total
    high, low = halves(total)
    removed = dot(turned_high[...], high) + (dot(turned_low[...], high) + dot(turned_high[...], low))
    remainder[...] = (placed_in[...] + add_placed) - removed


def mix_call(kernel, group, extra, turned, pieces, spots, q_high, q_low, targets, front_rows, tokens):
    panel = q_high.shape[0]
    block_cols = pieces[0].shape[1]
    depth = sum(size for _, _, size in spots)
    column = lambda j: (0, j)
    fixed = lambda j: (0, group)
    still = lambda j: (0, 0)
    flops = depth * block_cols * (3 * panel + 2 * front_rows)
    flops += 3 * panel * front_rows * block_cols if turned else 0
    return pl.pallas_call(
        functools.partial(kernel, len(pieces), spots),
        grid=(block_cols // WIDE,),
        out_shape=[
            jax.ShapeDtypeStruct((panel, block_cols), F32),
            jax.ShapeDtypeStruct((front_rows, block_cols), F32),
        ],
        in_specs=[
            pl.BlockSpec((panel, depth), fixed),
            pl.BlockSpec((panel, depth), fixed),
            pl.BlockSpec((1, depth), fixed),
        ]
        + [pl.BlockSpec((x.shape[0], WIDE), column) for x in extra]
        + [pl.BlockSpec(x.shape, still) for x in turned]
        + [pl.BlockSpec((x.shape[0], WIDE), column) for x in pieces]
        + [pl.BlockSpec(memory_space=pl.ANY)] * len(tokens),
        out_specs=[
            pl.BlockSpec((panel, WIDE), column),
            pl.BlockSpec((front_rows, WIDE), column),
        ],
        scratch_shapes=[pltpu.VMEM((front_rows, depth), BF16)],
        compiler_params=params(63),
        cost_estimate=pl.CostEstimate(
            flops=flops,
            bytes_accessed=block_cols * (depth + (1 + bool(extra)) * (panel + front_rows)),
            transcendentals=0,
        ),
    )(q_high, q_low, targets, *extra, *turned, *pieces, *tokens)


def shards(children, row_map, column_map, staircase):
    n_rt, n_ct = lax.axis_size("rt"), lax.axis_size("ct")
    my_rt, my_ct = lax.axis_index("rt"), lax.axis_index("ct")
    src, child_cols = children.shape
    total_rows = row_map.shape[0]
    child_rows = total_rows // 2
    front_rows = total_rows // n_rt
    tile_cols = child_cols // staircase.shape[1]
    n_dev = n_rt * n_ct

    first_row = (my_rt * n_ct + my_ct) * src
    which = first_row // child_rows
    first_within = first_row - which * child_rows
    cmap = lax.dynamic_index_in_dim(column_map, which, 0, keepdims=False)
    stairs = lax.dynamic_index_in_dim(staircase, which, 0, keepdims=False)
    limits = jnp.broadcast_to(stairs[:, None], (stairs.shape[0], tile_cols)).reshape(-1)

    edges = STEP * jnp.arange(FRONT_COLS // STEP, dtype=jnp.int32)
    starts = jnp.sum((cmap[None, :] < edges[:, None]).astype(jnp.int32), axis=1)
    starts = jnp.minimum(starts // LANES, (child_cols - STEP - LANES) // LANES)
    info = jnp.concatenate([starts, my_ct[None], first_within[None]]).astype(jnp.int32)
    two, eight = n_ct // 2, n_ct // 8
    near = sorted(range(1, two), key=lambda d: d % 2)
    near = [near[: -2 * eight], near[-2 * eight : -eight], near[-eight:]]
    far = [list(range(two + k * eight, two + (k + 1) * eight)) for k in range(4)]
    order = [0] + near[0] + far[0] + near[1] + far[1] + near[2] + far[2] + far[3]
    spread = functools.partial(widen, info, children, cmap[None, :], limits[None, :], n_ct=n_ct)
    ones = lambda groups: [(d, 1) for group in groups for d in group]
    blocks, mark = spread(ones([near[0]]), tokens=[])

    within = first_within + jnp.arange(src, dtype=jnp.int32)
    panel = jnp.where(within[:, None] < limits[None, :PANEL], children[:, :PANEL], 0.0)
    ct_bits, rt_bits = bits_down(n_ct, 1), bits_down(n_rt, 2)

    rt_order = combos(rt_bits)
    rt_order = rt_order + [r ^ 1 for r in rt_order]
    sources = (my_rt ^ np.array(rt_order, np.int32))[None, :] * n_ct + (
        my_ct ^ np.array(order, np.int32)
    )[:, None]
    targets = row_map.reshape(n_dev, src)[sources.reshape(-1)] - my_rt * front_rows
    targets = targets.reshape(n_ct, 1, n_rt * src)
    flat_targets = targets.reshape(1, total_rows)

    half = n_rt // 2

    def over_ct(group, tokens, part=0):
        operands = gate([blocks[d, part] for d in group], tokens)
        return [swap(x, 0, d) for d, x in zip(group, operands)]

    def over_rt(mine):
        mine = [mine]
        for bit in rt_bits:
            mine = mine + [swap(x, bit, 0) for x in mine]
        return mine

    def one(arrays):
        return arrays[0] if len(arrays) == 1 else join(arrays)[0]

    parts = [panel] + [swap(panel, 0, bits) for bits in combos(ct_bits[:-1])[1:]]
    for bit in rt_bits[:-1]:
        panel, _ = join(parts)
        parts = [panel, swap(panel, bit, 0)]
    (left, right), mark = join(parts, [mark], cut=2)
    near_a = over_ct(near[0], [mark])
    later = ones([[0]] + near[1:] + far[1:]) + [(d, 2) for d in far[0]]
    more, after = spread(later, tokens=[mark])
    blocks |= more
    left, mark = join([left, swap(left, rt_bits[-1], 0)], [after])
    right, _ = join([right, swap(right, 0, ct_bits[-1])])
    far_a = over_ct(far[0], [mark])
    left_other, right_other = swap(left, 0, ct_bits[-1]), swap(right, rt_bits[-1], 0)
    panel, gram, mark = gram_of(left, left_other, right, right_other, near_a + far_a)
    other_gram, other_panel = swap(gram, 1, 0), swap(panel, 1, 0)
    far_e = over_ct(far[0], [mark], 1)
    far_b, near_b = over_ct(far[1], [mark]), over_ct(near[1], [mark])
    joined, after = join([blocks[0, 0]] + near_a + far_a, [mark])
    first = over_rt(joined)
    inverse, mark = inverse_factor(gram, other_gram, [other_panel, after])

    late = list(gate(first + near_b + far_e + far_b, [mark]))
    first, late = late[:half], late[half:]
    far_c, near_c = over_ct(far[2], late[:1]), over_ct(near[2], late[:1])
    joined, mark = join(late[eight : 2 * eight] + late[:eight] + late[2 * eight :])
    second = over_rt(joined)
    crossed = swap(first[0], 1, 0)
    inverse = [inverse]
    q_high, q_low, basis, turned_high, turned_low = basis_rows(
        inverse,
        panel.reshape(2, half, n_ct // 2, src, PANEL),
        other_panel.reshape(2, half, n_ct // 2, src, PANEL),
        targets,
        [mark],
        front_rows,
        order,
    )

    call = functools.partial(mix_call, q_high=q_high, q_low=q_low, targets=flat_targets, front_rows=front_rows)
    late = list(gate(first + [crossed] + second + near_c + far_c, [basis]))
    crossed = late.pop(half)
    first, second, late = late[:half], late[half : 2 * half], late[2 * half :]
    far_d = over_ct(far[3], late[:1])
    third, fourth = over_rt(one(late[:eight])), over_rt(one(late[eight:]))
    first += [crossed] + [swap(x, 1, 0) for x in first[1:]]
    second += [swap(x, 1, 0) for x in second]

    def rows_of(mine, start, size):
        return [(mine + n, start, size) for n in range(n_rt)]

    def group(bundles):
        arrays, spots = [], []
        for mine in bundles:
            for row in range(0, mine[0].shape[0], src):
                spots += rows_of(len(arrays), row, src)
            arrays += mine
        return tuple(arrays), tuple(spots)

    part, height = src // 2, first[0].shape[0]
    whole_rows = height - part * eight
    places = [(n, 0) for n in range(n_rt)]
    spots = [(side, at + row, src) for row in range(0, whole_rows, src) for side, at in places]
    for k in range(eight):
        for n, (side, at) in enumerate(places):
            spots += [(side, at + whole_rows + k * part, part), (n_rt + n, k * part, part)]
    for row in range(part * eight, second[0].shape[0], src):
        spots += rows_of(n_rt, row, src)
    arrays = tuple(first) + tuple(second)
    state = call(first_kernel, 0, (), (), arrays, tuple(spots), tokens=late[:1])
    late = list(gate(third + fourth + far_d, [state[0]]))
    third, fourth, late = late[:half], late[half : 2 * half], late[2 * half :]
    fifth = over_rt(one(late))
    third += [swap(x, 1, 0) for x in third]
    fourth += [swap(x, 1, 0) for x in fourth]
    state = call(more_kernel, 5, tuple(state), (), *group((third,)), tokens=fourth[half:])
    fifth = list(gate(fifth, [state[0]]))
    fifth += [swap(x, 1, 0) for x in fifth]
    turned = (turned_high, turned_low)
    factor, remainder = call(last_kernel, 3, tuple(state), turned, *group((fourth, fifth)), tokens=[])
    return factor, basis, remainder


def solution(mesh):
    placed = (P(("rt", "ct"), None), P(), P(), P())
    return jax.shard_map(
        shards,
        mesh=mesh,
        in_specs=placed,
        out_specs=(P(None, "ct"), P(None, "rt"), P("rt", "ct")),
        check_vma=False,
    )
```

```python
import functools

import jax
import jax.numpy as jnp
import numpy as np
from jax import lax
from jax.experimental import pallas as pl
from jax.experimental.pallas import tpu as pltpu
from jax.sharding import PartitionSpec as P

FRONT_COLS = 16384
PANEL = 512
STEP = 256
WIDE = 1024
UNROLL = 8
LANES = 128
NB = 128
SUB = 8

HI = lax.Precision.HIGHEST
F32 = jnp.float32
BF16 = jnp.bfloat16
MIB = 2**20


def swap(x, rt_bit, ct_bit):
    n_rt, n_ct = lax.axis_size("rt"), lax.axis_size("ct")
    if not rt_bit:
        return lax.ppermute(x, "ct", [(c, c ^ ct_bit) for c in range(n_ct)])
    if not ct_bit:
        return lax.ppermute(x, "rt", [(r, r ^ rt_bit) for r in range(n_rt)])
    pairs = [
        (r * n_ct + c, (r ^ rt_bit) * n_ct + (c ^ ct_bit)) for r in range(n_rt) for c in range(n_ct)
    ]
    return lax.ppermute(x, ("rt", "ct"), pairs)


def bits_down(size, last):
    bit, bits = size // 2, []
    while bit >= last:
        bits.append(bit)
        bit //= 2
    return bits


def combos(bits):
    order = [0]
    for bit in bits:
        order = order + [value ^ bit for value in order]
    return order


def halves(x):
    high = x.astype(BF16)
    return high, (x - high.astype(F32)).astype(BF16)


def dot(a, b):
    return jnp.dot(a, b, preferred_element_type=F32)


def dot_nt(a, b, precision=None):
    return lax.dot_general(
        a, b, (((1,), (1,)), ((), ())), precision=precision, preferred_element_type=F32
    )


def dot_tn(a, b, precision=None):
    return lax.dot_general(
        a, b, (((0,), (0,)), ((), ())), precision=precision, preferred_element_type=F32
    )


MARK = jax.ShapeDtypeStruct((SUB, LANES), F32)


def params(mib):
    return pltpu.CompilerParams(vmem_limit_bytes=mib * MIB)


def widen_kernel(tiles, window, places, waits, info, child, cmap, limits, *outs):
    rows = child.shape[0]
    my_block = info[info.shape[0] - 2]
    first_row = info[info.shape[0] - 1]
    row_ids = first_row + lax.broadcasted_iota(jnp.int32, (rows, window), 0)
    col_ids = lax.broadcasted_iota(jnp.int32, (STEP, window), 0)
    made = iter(outs[waits:-1])
    for place, cut in places:
        block = my_block ^ place
        parts = [next(made) for _ in range(cut)]

        def tile(i, carry, block=block, parts=parts):
            t = block * tiles + i
            cols = pl.ds(pl.multiple_of(info[t] * LANES, LANES), window)
            live = jnp.where(row_ids < limits[:, cols], child[:, cols], 0.0)
            hot = jnp.where(col_ids == cmap[:, cols] - t * STEP, 1.0, 0.0).astype(BF16)
            spread = dot_nt(jnp.concatenate(halves(live), axis=0), hot)
            spread = spread[:rows] + spread[rows:]
            there = pl.ds(pl.multiple_of(i * STEP, STEP), STEP)
            height = rows // len(parts)
            for k, part in enumerate(parts):
                part[:, there] = spread[k * height : (k + 1) * height]
            return carry

        lax.fori_loop(0, tiles, tile, 0, unroll=UNROLL)


def widen(info, child, cmap, limits, places, n_ct, tokens):
    rows, width = child.shape
    block_cols = FRONT_COLS // n_ct
    window = STEP + LANES
    whole = pl.BlockSpec(memory_space=pltpu.VMEM)
    made = pl.pallas_call(
        functools.partial(widen_kernel, block_cols // STEP, window, tuple(places), len(tokens)),
        out_shape=[
            jax.ShapeDtypeStruct((rows // cut, block_cols), F32)
            for _, cut in places
            for _ in range(cut)
        ]
        + [MARK],
        in_specs=[pl.BlockSpec(memory_space=pltpu.SMEM), whole, whole, whole]
        + [pl.BlockSpec(memory_space=pl.ANY)] * len(tokens),
        out_specs=[whole] * sum(cut for _, cut in places) + [pl.BlockSpec(memory_space=pl.ANY)],
        compiler_params=params(63),
        cost_estimate=pl.CostEstimate(
            flops=4 * rows * window * block_cols * len(places),
            bytes_accessed=4 * rows * (width + block_cols * len(places)),
            transcendentals=0,
        ),
    )(info, child, cmap, limits, *tokens)
    keys = [(d, k) for d, cut in places for k in range(cut)]
    return dict(zip(keys, made)), made[-1]


def small_inverse(tile):
    a = [
        [jnp.broadcast_to(tile[i : i + 1, k : k + 1], (SUB, NB)) for k in range(i + 1)]
        for i in range(SUB)
    ]
    scale = [None] * SUB
    lower = [[None] * SUB for _ in range(SUB)]
    inverse = [[None] * SUB for _ in range(SUB)]
    for j in range(SUB):
        scale[j] = lax.rsqrt(a[j][j])
        for i in range(j + 1, SUB):
            lower[i][j] = a[i][j] * scale[j]
        for i in range(j + 1, SUB):
            for k in range(j + 1, i + 1):
                a[i][k] = a[i][k] - lower[i][j] * lower[k][j]
    for j in range(SUB):
        inverse[j][j] = scale[j]
        for i in range(j + 1, SUB):
            total = lower[i][j] * inverse[j][j]
            for k in range(j + 1, i):
                total = total + lower[i][k] * inverse[k][j]
            inverse[i][j] = -scale[i] * total
    return inverse


def apply_small(inverse, tiles):
    sub = lax.broadcasted_iota(jnp.int32, (SUB, NB), 0)
    outs = [None] * len(tiles)
    for k in range(SUB):
        column = jnp.zeros((SUB, NB), F32)
        for i in range(k, SUB):
            column = jnp.where(sub == i, inverse[i][k], column)
        for n, tile in enumerate(tiles):
            term = column * jnp.broadcast_to(tile[k : k + 1, :], (SUB, NB))
            outs[n] = term if outs[n] is None else outs[n] + term
    return outs


def identity(n):
    shape = (n, n)
    same = lax.broadcasted_iota(jnp.int32, shape, 0) == lax.broadcasted_iota(jnp.int32, shape, 1)
    return jnp.where(same, 1.0, 0.0)


def thirds(x):
    high = x.astype(BF16)
    rest = x - high.astype(F32)
    mid = rest.astype(BF16)
    return high, mid, (rest - mid.astype(F32)).astype(BF16)


def diagonal_inverse(block, out, work):
    lane = lax.broadcasted_iota(jnp.int32, (SUB, NB), 1)
    work[:NB, :NB] = block
    work[:NB, NB:] = identity(NB)
    work[NB:, :] = jnp.zeros((SUB, 2 * NB), F32)

    def body(s, carry):
        tile, before = carry
        h, m, l = thirds(before)
        left = jnp.concatenate([x[:, :NB] for x in (h, h, m, h, l, m)], axis=0)
        right = jnp.concatenate([h, m, h, l, h, m], axis=0)
        work[:NB, :] = work[:NB, :] - dot_tn(left, right)
        after = work[pl.ds(pl.multiple_of(SUB * s + SUB, SUB), SUB), :]
        shift = lax.rem(NB - SUB * s, NB)
        inverse = small_inverse(pltpu.roll(tile[:, :NB], shift, 1))
        turned = pltpu.roll(after[:, :NB], shift, 1)
        top, top_right = apply_small(inverse, [tile[:, :NB], tile[:, NB:]])
        out[pl.ds(pl.multiple_of(SUB * s, SUB), SUB), :] = top_right
        top = jnp.concatenate([jnp.where(lane >= SUB * s, top, 0.0), top_right], axis=1)
        columns = [jnp.broadcast_to(turned[:, k : k + 1], (SUB, NB)) for k in range(SUB)]
        for i in range(SUB):
            weight = inverse[i][0] * columns[0]
            for k in range(1, i + 1):
                weight = weight + inverse[i][k] * columns[k]
            weight = jnp.concatenate([weight, weight], axis=1)
            after = after - weight * jnp.broadcast_to(top[i : i + 1], (SUB, 2 * NB))
        return after, top

    start = (work[:SUB, :], jnp.zeros((SUB, 2 * NB), F32))
    lax.fori_loop(0, NB // SUB, body, start, unroll=2)


def factor_kernel(gram_a, gram_b, *refs):
    out, _, whole, small, work = refs[-5:]
    n = out.shape[0]
    whole[:, :n] = gram_a[...] + gram_b[...]
    whole[:, n:] = identity(n)
    for lo in range(0, n, NB):
        hi = lo + NB
        diagonal_inverse(whole[lo:hi, lo:hi], small, work)
        rows = jnp.dot(small[...], whole[lo:hi, lo : n + hi], precision=HI, preferred_element_type=F32)
        out[lo:hi, :hi] = rows[:, n - lo :]
        if hi < n:
            out[lo:hi, hi:] = jnp.zeros((NB, n - hi), F32)
            whole[hi:, hi : n + hi] -= dot_tn(rows[:, NB : n - lo], rows[:, NB:], HI)


def inverse_factor(gram_a, gram_b, tokens):
    n = gram_a.shape[0]
    whole = pl.BlockSpec(memory_space=pltpu.VMEM)
    return pl.pallas_call(
        factor_kernel,
        out_shape=[jax.ShapeDtypeStruct((n, n), F32), MARK],
        in_specs=[whole] * 2 + [pl.BlockSpec(memory_space=pl.ANY)] * len(tokens),
        out_specs=[whole, pl.BlockSpec(memory_space=pl.ANY)],
        scratch_shapes=[
            pltpu.VMEM((n, 2 * n), F32),
            pltpu.VMEM((NB, NB), F32),
            pltpu.VMEM((NB + SUB, 2 * NB), F32),
        ],
        compiler_params=params(63),
        cost_estimate=pl.CostEstimate(
            flops=30 * 10**9, bytes_accessed=12 * n * n, transcendentals=0
        ),
    )(gram_a, gram_b, *tokens)


def gate_kernel(*refs):
    pass


def gate(arrays, tokens):
    if not arrays:
        return []
    anywhere = pl.BlockSpec(memory_space=pl.ANY)
    return pl.pallas_call(
        gate_kernel,
        out_shape=[jax.ShapeDtypeStruct(x.shape, x.dtype) for x in arrays],
        in_specs=[anywhere] * (len(arrays) + len(tokens)),
        out_specs=[anywhere] * len(arrays),
        input_output_aliases={k: k for k in range(len(arrays))},
        cost_estimate=pl.CostEstimate(flops=0, bytes_accessed=0, transcendentals=0),
    )(*arrays, *tokens)


def join_kernel(count, cut, *refs):
    parts, outs = refs[:count], refs[-cut - 1 : -1]
    width = outs[0].shape[1]
    row = 0
    for part in parts:
        rows = part.shape[0]
        for k, out in enumerate(outs):
            out[row : row + rows, :] = part[:, k * width : (k + 1) * width]
        row += rows


def join(parts, tokens=(), cut=1):
    rows, width = sum(x.shape[0] for x in parts), parts[0].shape[1]
    whole = pl.BlockSpec(memory_space=pltpu.VMEM)
    out = pl.pallas_call(
        functools.partial(join_kernel, len(parts), cut),
        out_shape=[jax.ShapeDtypeStruct((rows, width // cut), F32)] * cut + [MARK],
        in_specs=[whole] * len(parts) + [pl.BlockSpec(memory_space=pl.ANY)] * len(tokens),
        out_specs=[whole] * cut + [pl.BlockSpec(memory_space=pl.ANY)],
        compiler_params=params(16 if width <= PANEL else 63),
        cost_estimate=pl.CostEstimate(
            flops=0, bytes_accessed=8 * rows * width, transcendentals=0
        ),
    )(*parts, *tokens)
    return (out[:cut] if cut > 1 else out[0]), out[-1]


def gram_kernel(a_mine, a_other, b_mine, b_other, *refs):
    panel, gram = refs[-3:-1]
    half, width = a_mine.shape
    quarter = half // 2
    panel[:half, :width] = a_mine[...]
    panel[half:, :width] = a_other[...]
    for k, source in enumerate((b_mine, b_other)):
        panel[k * quarter : (k + 1) * quarter, width:] = source[:quarter, :]
        panel[half + k * quarter : half + (k + 1) * quarter, width:] = source[quarter:, :]
    rows = panel[...]
    gram[...] = dot_tn(rows, rows, HI)


def gram_of(a_mine, a_other, b_mine, b_other, tokens):
    half, width = a_mine.shape
    whole = pl.BlockSpec(memory_space=pltpu.VMEM)
    return pl.pallas_call(
        gram_kernel,
        out_shape=[
            jax.ShapeDtypeStruct((2 * half, 2 * width), F32),
            jax.ShapeDtypeStruct((2 * width, 2 * width), F32),
            MARK,
        ],
        in_specs=[whole] * 4 + [pl.BlockSpec(memory_space=pl.ANY)] * len(tokens),
        out_specs=[whole] * 2 + [pl.BlockSpec(memory_space=pl.ANY)],
        compiler_params=params(24),
        cost_estimate=pl.CostEstimate(
            flops=4 * half * 4 * width * width, bytes_accessed=4 * half * width, transcendentals=0
        ),
    )(a_mine, a_other, b_mine, b_other, *tokens)


def basis_kernel(count, waits, *refs):
    inverse, refs = refs[:count], refs[count:]
    own, other, targets = refs[:3]
    q_high, q_low, basis, turned_high, turned_low = refs[3 + waits :]
    d = pl.program_id(0)
    group, panel = targets.shape[-1], inverse[0].shape[1]
    rows = jnp.concatenate(
        [own[...].reshape(group // 2, panel), other[...].reshape(group // 2, panel)], axis=0
    )
    inv_high, inv_low = halves(inverse[0][...])
    high, low = halves(rows)
    q = dot_nt(inv_high, high) + (dot_nt(inv_low, high) + dot_nt(inv_high, low))
    q_h, q_l = halves(q)
    q_high[...] = q_h
    q_low[...] = q_l
    front = basis.shape[1]
    ids = lax.broadcasted_iota(jnp.int32, (front, group), 0)
    hot = jnp.where(ids == targets[0], 1.0, 0.0).astype(BF16)
    part = dot_nt(q_h, hot) + dot_nt(q_l, hot)

    @pl.when(d == 0)
    def _():
        basis[...] = part

    @pl.when(d > 0)
    def _():
        basis[...] += part

    @pl.when(d == pl.num_programs(0) - 1)
    def _():
        turned_h, turned_l = halves(basis[...].T)
        turned_high[...] = turned_h
        turned_low[...] = turned_l


def basis_rows(inverse, own, other, targets, tokens, front_rows, order):
    last, half, upper, src, panel = own.shape
    n_ct = last * upper
    group = 2 * half * src
    depth = upper.bit_length() - 1

    def place(step):
        d = sum(jnp.where(step == k, value, 0) for k, value in enumerate(order))
        spot = sum(((d >> (k + 1)) & 1) << (depth - 1 - k) for k in range(depth))
        return (d & 1, 0, spot, 0, 0)

    wide = jax.ShapeDtypeStruct((panel, n_ct * group), BF16)
    return pl.pallas_call(
        functools.partial(basis_kernel, len(inverse), len(tokens)),
        grid=(n_ct,),
        out_shape=[
            wide,
            wide,
            jax.ShapeDtypeStruct((panel, front_rows), F32),
            jax.ShapeDtypeStruct((front_rows, panel), BF16),
            jax.ShapeDtypeStruct((front_rows, panel), BF16),
        ],
        in_specs=[
            *[pl.BlockSpec((panel, panel), lambda d: (0, 0)) for _ in inverse],
            pl.BlockSpec((1, half, 1, src, panel), place),
            pl.BlockSpec((1, half, 1, src, panel), place),
            pl.BlockSpec((1, 1, group), lambda d: (d, 0, 0)),
            *[pl.BlockSpec(memory_space=pl.ANY) for _ in tokens],
        ],
        out_specs=[
            pl.BlockSpec((panel, group), lambda d: (0, d)),
            pl.BlockSpec((panel, group), lambda d: (0, d)),
            pl.BlockSpec((panel, front_rows), lambda d: (0, 0)),
            pl.BlockSpec((front_rows, panel), lambda d: (0, 0)),
            pl.BlockSpec((front_rows, panel), lambda d: (0, 0)),
        ],
        compiler_params=params(63),
        cost_estimate=pl.CostEstimate(
            flops=8 * panel * panel * n_ct * group, bytes_accessed=6 * MIB, transcendentals=0
        ),
    )(*inverse, own, other, targets, *tokens)


def mix(q_high, q_low, hot, pieces, spots):
    rows = jnp.concatenate([pieces[n][lo : lo + size, :] for n, lo, size in spots], axis=0)
    high, low = halves(rows)
    factor = dot(q_high[...], high) + (dot(q_low[...], high) + dot(q_high[...], low))
    return factor, dot(hot[...], high) + dot(hot[...], low)


def build_hot(targets, hot):
    @pl.when(pl.program_id(0) == 0)
    def _():
        ids = lax.broadcasted_iota(jnp.int32, hot.shape, 0)
        hot[...] = jnp.where(ids == targets[...], 1.0, 0.0).astype(BF16)


def first_kernel(count, spots, q_high, q_low, targets, *refs):
    pieces, (factor, placed, hot) = refs[:count], refs[-3:]
    build_hot(targets, hot)
    factor[...], placed[...] = mix(q_high, q_low, hot, pieces, spots)


def more_kernel(count, spots, q_high, q_low, targets, factor_in, placed_in, *refs):
    pieces, (factor, placed, hot) = refs[:count], refs[-3:]
    build_hot(targets, hot)
    add_factor, add_placed = mix(q_high, q_low, hot, pieces, spots)
    factor[...] = factor_in[...] + add_factor
    placed[...] = placed_in[...] + add_placed


def last_kernel(count, spots, q_high, q_low, targets, factor_in, placed_in, turned_high, turned_low, *refs):
    pieces, (factor, remainder, hot) = refs[:count], refs[-3:]
    build_hot(targets, hot)
    add_factor, add_placed = mix(q_high, q_low, hot, pieces, spots)
    total = factor_in[...] + add_factor
    factor[...] = total
    high, low = halves(total)
    removed = dot(turned_high[...], high) + (dot(turned_low[...], high) + dot(turned_high[...], low))
    remainder[...] = (placed_in[...] + add_placed) - removed


def mix_call(kernel, group, extra, turned, pieces, spots, q_high, q_low, targets, front_rows, tokens):
    panel = q_high.shape[0]
    block_cols = pieces[0].shape[1]
    depth = sum(size for _, _, size in spots)
    column = lambda j: (0, j)
    fixed = lambda j: (0, group)
    still = lambda j: (0, 0)
    flops = depth * block_cols * (3 * panel + 2 * front_rows)
    flops += 3 * panel * front_rows * block_cols if turned else 0
    return pl.pallas_call(
        functools.partial(kernel, len(pieces), spots),
        grid=(block_cols // WIDE,),
        out_shape=[
            jax.ShapeDtypeStruct((panel, block_cols), F32),
            jax.ShapeDtypeStruct((front_rows, block_cols), F32),
        ],
        in_specs=[
            pl.BlockSpec((panel, depth), fixed),
            pl.BlockSpec((panel, depth), fixed),
            pl.BlockSpec((1, depth), fixed),
        ]
        + [pl.BlockSpec((x.shape[0], WIDE), column) for x in extra]
        + [pl.BlockSpec(x.shape, still) for x in turned]
        + [pl.BlockSpec((x.shape[0], WIDE), column) for x in pieces]
        + [pl.BlockSpec(memory_space=pl.ANY)] * len(tokens),
        out_specs=[
            pl.BlockSpec((panel, WIDE), column),
            pl.BlockSpec((front_rows, WIDE), column),
        ],
        scratch_shapes=[pltpu.VMEM((front_rows, depth), BF16)],
        compiler_params=params(63),
        cost_estimate=pl.CostEstimate(
            flops=flops,
            bytes_accessed=block_cols * (depth + (1 + bool(extra)) * (panel + front_rows)),
            transcendentals=0,
        ),
    )(q_high, q_low, targets, *extra, *turned, *pieces, *tokens)


def shards(children, row_map, column_map, staircase):
    n_rt, n_ct = lax.axis_size("rt"), lax.axis_size("ct")
    my_rt, my_ct = lax.axis_index("rt"), lax.axis_index("ct")
    src, child_cols = children.shape
    total_rows = row_map.shape[0]
    child_rows = total_rows // 2
    front_rows = total_rows // n_rt
    tile_cols = child_cols // staircase.shape[1]
    n_dev = n_rt * n_ct

    first_row = (my_rt * n_ct + my_ct) * src
    which = first_row // child_rows
    first_within = first_row - which * child_rows
    cmap = lax.dynamic_index_in_dim(column_map, which, 0, keepdims=False)
    stairs = lax.dynamic_index_in_dim(staircase, which, 0, keepdims=False)
    limits = jnp.broadcast_to(stairs[:, None], (stairs.shape[0], tile_cols)).reshape(-1)

    edges = STEP * jnp.arange(FRONT_COLS // STEP, dtype=jnp.int32)
    starts = jnp.sum((cmap[None, :] < edges[:, None]).astype(jnp.int32), axis=1)
    starts = jnp.minimum(starts // LANES, (child_cols - STEP - LANES) // LANES)
    info = jnp.concatenate([starts, my_ct[None], first_within[None]]).astype(jnp.int32)
    two, eight = n_ct // 2, n_ct // 8
    near = sorted(range(1, two), key=lambda d: d % 2)
    near = [near[: -2 * eight], near[-2 * eight : -eight], near[-eight:]]
    far = [list(range(two + k * eight, two + (k + 1) * eight)) for k in range(4)]
    order = [0] + near[0] + far[0] + near[1] + far[1] + near[2] + far[2] + far[3]
    spread = functools.partial(widen, info, children, cmap[None, :], limits[None, :], n_ct=n_ct)
    ones = lambda groups: [(d, 1) for group in groups for d in group]
    blocks, mark = spread(ones([near[0]]), tokens=[])

    within = first_within + jnp.arange(src, dtype=jnp.int32)
    panel = jnp.where(within[:, None] < limits[None, :PANEL], children[:, :PANEL], 0.0)
    ct_bits, rt_bits = bits_down(n_ct, 1), bits_down(n_rt, 2)

    rt_order = combos(rt_bits)
    rt_order = rt_order + [r ^ 1 for r in rt_order]
    sources = (my_rt ^ np.array(rt_order, np.int32))[None, :] * n_ct + (
        my_ct ^ np.array(order, np.int32)
    )[:, None]
    targets = row_map.reshape(n_dev, src)[sources.reshape(-1)] - my_rt * front_rows
    targets = targets.reshape(n_ct, 1, n_rt * src)
    flat_targets = targets.reshape(1, total_rows)

    half = n_rt // 2

    def over_ct(group, tokens, part=0):
        operands = gate([blocks[d, part] for d in group], tokens)
        return [swap(x, 0, d) for d, x in zip(group, operands)]

    def over_rt(mine):
        mine = [mine]
        for bit in rt_bits:
            mine = mine + [swap(x, bit, 0) for x in mine]
        return mine

    def one(arrays):
        return arrays[0] if len(arrays) == 1 else join(arrays)[0]

    parts = [panel] + [swap(panel, 0, bits) for bits in combos(ct_bits[:-1])[1:]]
    for bit in rt_bits[:-1]:
        panel, _ = join(parts)
        parts = [panel, swap(panel, bit, 0)]
    (left, right), mark = join(parts, [mark], cut=2)
    near_a = over_ct(near[0], [mark])
    later = ones([[0]] + near[1:] + far[1:]) + [(d, 2) for d in far[0]]
    more, after = spread(later, tokens=[mark])
    blocks |= more
    left, mark = join([left, swap(left, rt_bits[-1], 0)], [after])
    right, _ = join([right, swap(right, 0, ct_bits[-1])])
    far_a = over_ct(far[0], [mark])
    left_other, right_other = swap(left, 0, ct_bits[-1]), swap(right, rt_bits[-1], 0)
    panel, gram, mark = gram_of(left, left_other, right, right_other, near_a + far_a)
    other_gram, other_panel = swap(gram, 1, 0), swap(panel, 1, 0)
    far_e = over_ct(far[0], [mark], 1)
    far_b, near_b = over_ct(far[1], [mark]), over_ct(near[1], [mark])
    joined, after = join([blocks[0, 0]] + near_a + far_a, [mark])
    first = over_rt(joined)
    inverse, mark = inverse_factor(gram, other_gram, [other_panel, after])

    late = list(gate(first + near_b + far_e + far_b, [mark]))
    first, late = late[:half], late[half:]
    far_c, near_c = over_ct(far[2], late[:1]), over_ct(near[2], late[:1])
    joined, mark = join(late[eight : 2 * eight] + late[:eight] + late[2 * eight :])
    second = over_rt(joined)
    crossed = swap(first[0], 1, 0)
    inverse = [inverse]
    q_high, q_low, basis, turned_high, turned_low = basis_rows(
        inverse,
        panel.reshape(2, half, n_ct // 2, src, PANEL),
        other_panel.reshape(2, half, n_ct // 2, src, PANEL),
        targets,
        [mark],
        front_rows,
        order,
    )

    call = functools.partial(mix_call, q_high=q_high, q_low=q_low, targets=flat_targets, front_rows=front_rows)
    late = list(gate(first + [crossed] + second + near_c + far_c, [basis]))
    crossed = late.pop(half)
    first, second, late = late[:half], late[half : 2 * half], late[2 * half :]
    far_d = over_ct(far[3], late[:1])
    third, fourth = over_rt(one(late[:eight])), over_rt(one(late[eight:]))
    first += [crossed] + [swap(x, 1, 0) for x in first[1:]]
    second += [swap(x, 1, 0) for x in second]

    def rows_of(mine, start, size):
        return [(mine + n, start, size) for n in range(n_rt)]

    def group(bundles):
        arrays, spots = [], []
        for mine in bundles:
            for row in range(0, mine[0].shape[0], src):
                spots += rows_of(len(arrays), row, src)
            arrays += mine
        return tuple(arrays), tuple(spots)

    part, height = src // 2, first[0].shape[0]
    whole_rows = height - part * eight
    places = [(n, 0) for n in range(n_rt)]
    spots = [(side, at + row, src) for row in range(0, whole_rows, src) for side, at in places]
    for k in range(eight):
        for n, (side, at) in enumerate(places):
            spots += [(side, at + whole_rows + k * part, part), (n_rt + n, k * part, part)]
    for row in range(part * eight, second[0].shape[0], src):
        spots += rows_of(n_rt, row, src)
    arrays = tuple(first) + tuple(second)
    state = call(first_kernel, 0, (), (), arrays, tuple(spots), tokens=late[:1])
    late = list(gate(third + fourth + far_d, [state[0]]))
    third, fourth, late = late[:half], late[half : 2 * half], late[2 * half :]
    fifth = over_rt(one(late))
    third += [swap(x, 1, 0) for x in third]
    fourth += [swap(x, 1, 0) for x in fourth]
    state = call(more_kernel, 5, tuple(state), (), *group((third,)), tokens=fourth[half:])
    fifth = list(gate(fifth, [state[0]]))
    fifth += [swap(x, 1, 0) for x in fifth]
    turned = (turned_high, turned_low)
    factor, remainder = call(last_kernel, 3, tuple(state), turned, *group((fourth, fifth)), tokens=[])
    return factor, basis, remainder


def solution(mesh):
    placed = (P(("rt", "ct"), None), P(), P(), P())
    return jax.shard_map(
        shards,
        mesh=mesh,
        in_specs=placed,
        out_specs=(P(None, "ct"), P(None, "rt"), P("rt", "ct")),
        check_vma=False,
    )
```
